128 devices in a mesh: comp: 2 (over core), dom: 64 (over y, z, x).
Axes of the slice: x: 4, y: 4, z: 4, core: 2. Of those that a mesh axis runs over, the one named last changes fastest.
Arguments:
- column_state: float32 [2, 8, 16, 131072], P('comp', None, None, 'dom'), may hold values from -6 to 6
- vert_rate: float32 [2, 7, 131072], P('comp', None, 'dom'), may hold values from 0.03 to 0.4
- hor_offsets: int32 [2, 6, 131072], P('comp', None, 'dom'), may hold values from -512 to 512, as said below
- hor_coef: float32 [2, 6, 131072], P('comp', None, 'dom'), may hold values from 0.01 to 0.15
- open_mask: int32 [2, 131072], P('comp', 'dom'), may hold values 0 or 1
- couple_rate: float32 [2, 16], P('comp'), may hold values from 0.2 to 0.9
- send_index: int32 [2, 64, 5, 4, 256], P('comp', 'dom'), may hold values from 0 to 2047
- live_slots: int32 [2, 64, 5], P('comp', 'dom'), may hold values from 0 to 4, as said below
- block_source: int32 [2, 64, 8, 2], P('comp', 'dom'), may hold values from 0 to 19
- remap_weight: bfloat16 [2, 64, 8, 2, 256, 256], P('comp', 'dom')
Outputs:
- new_state: float32 [2, 8, 16, 131072], P('comp', None, None, 'dom')
- forcing: float32 [2, 16, 131072], P('comp', None, 'dom')
The draws below stay inside these ranges and needn't reach their ends.
Inputs may be any that keep to these rules, and one draw needn't show every extreme that they name: `send_index`: entries are column positions within the sending partition's 2048 columns. `hor_offsets`: offsets are nonzero and taken cyclically over the section's 131072 columns. `live_slots`: the pair at offset index 2 always uses all 4 slots.
All inputs are finite; a program needn't handle non-finite values. No bound on the sum of `open_mask` on one device may be relied on, other than what follows from the above.
Results may differ from the reference program's by a relative error of at most 0.0029.
Values may be sent and summed in bfloat16 or wider, within the bound.
No kernel may reach another device: no remote copies, remote signals or barrier semaphores. Data moves between devices by JAX's collectives and lax.ppermute only.
A program may use at most 128 MiB of HBM per device.

```python
import math
import jax
import jax.numpy as jnp
from jax import lax

F = 16
LEV = 8
COLS = 2048
BLKW = 256
TERMS = 2
RADIUS = 2
SLOTS = 4
RIM = 512
NSUB = 4
PARTNERS = 5
NB = 8
NCOL = 131072
N_DOM = 64


def draw_hor_offsets(key, part):
    key = jax.random.fold_in(key, 11)
    first_key, second_key = jax.random.split(key)
    magnitude = jax.random.randint(first_key, (2, 6, NCOL), 1, RIM + 1)
    direction = jax.random.randint(second_key, (2, 6, NCOL), 0, 2) * 2 - 1
    offsets = magnitude * direction
    offsets = offsets.at[:, 0, 0].set(RIM).at[:, 1, 0].set(-RIM)
    return offsets.astype(jnp.int32)


def draw_live_slots(key, part):
    key = jax.random.fold_in(key, 23)
    counts_drawn = jax.random.randint(key, (2, N_DOM, 2 * RADIUS + 1), 0, SLOTS + 1)
    counts_drawn = counts_drawn.at[:, :, RADIUS].set(SLOTS)
    return counts_drawn.astype(jnp.int32)


def draw_remap_weight(key, part):
    key = jax.random.fold_in(key, 37)
    uniform_draw = jax.random.uniform(key, (2, N_DOM, NB, TERMS, BLKW, BLKW), jnp.float32)
    weights = jnp.maximum(uniform_draw - 0.9, 0.0) * 10.0
    return weights.astype(jnp.bfloat16)


def plant(array, key, low, top_value):
    index_at = [jax.random.randint(jax.random.fold_in(key, axis), (), 0, length) for axis, length in enumerate(array.shape)]
    main_axis = array.shape.index(max(array.shape))
    neighbour = index_at[:main_axis] + [(index_at[main_axis] + 1) % array.shape[main_axis]] + index_at[main_axis + 1:]
    return array.at[tuple(index_at)].set(low).at[tuple(neighbour)].set(top_value)


def block_scale(key, dims, pieces, least, top_value):
    factor_of, own = 1.0, jax.random.fold_in(key, 6)
    for dim, shards_of in pieces:
        heights = jnp.exp(jax.random.uniform(jax.random.fold_in(own, dim), (shards_of,), jnp.float32, least / len(pieces), top_value / len(pieces)))
        factor_of = factor_of * jnp.repeat(heights, dims[dim] // shards_of).reshape([-1 if axis == dim else 1 for axis in range(len(dims))])
    return factor_of


def normal_values(stream_key, shape, width, most, pieces=(), kind=jnp.bfloat16):
    gain = block_scale(stream_key, shape, pieces, -0.22, 0.18) if pieces else 1.0
    array = jax.random.normal(stream_key, shape, jnp.float32) * width * gain
    return jnp.minimum(jnp.maximum(array, -most), most).astype(kind)


def setup_inputs(seed: int = 0) -> dict:
    streams_of = jax.random.split(jax.random.key(seed), 11)
    return {
        "column_state": normal_values(streams_of[0], (2, LEV, F, NCOL), 1.0, 6.0, ((0, 2), (3, 64)), jnp.float32),
        "vert_rate": jnp.clip(jnp.exp(math.log(0.4) - 2.5902672 * jax.random.uniform(streams_of[1], (2, LEV - 1, NCOL), jnp.float32) ** block_scale(streams_of[1], (2, LEV - 1, NCOL), ((0, 2), (2, 64)), -0.2, 0.2)), 0.03, 0.4),
        "hor_offsets": draw_hor_offsets(jax.random.fold_in(streams_of[10], 71), 0),
        "hor_coef": jnp.clip(jnp.exp(math.log(0.15) - 2.7080503 * jax.random.uniform(streams_of[3], (2, 6, NCOL), jnp.float32) ** block_scale(streams_of[3], (2, 6, NCOL), ((0, 2), (2, 64)), -0.2, 0.2)), 0.01, 0.15),
        "open_mask": plant((jax.random.randint(streams_of[4], (2, NCOL), 0, 3) < 2).astype(jnp.int32), jax.random.fold_in(streams_of[4], 1), 0, 1),
        "couple_rate": jnp.clip(0.2 + 0.7 * jax.random.uniform(streams_of[5], (2, F), jnp.float32) ** block_scale(streams_of[5], (2, F), ((0, 2),), -0.2, 0.2), 0.2, 0.9),
        "send_index": plant(jax.random.randint(streams_of[6], (2, N_DOM, PARTNERS, SLOTS, BLKW), 0, COLS), jax.random.fold_in(streams_of[6], 1), 0, COLS - 1).astype(jnp.int32),
        "live_slots": draw_live_slots(jax.random.fold_in(streams_of[10], 71), 0),
        "block_source": plant(jax.random.randint(streams_of[8], (2, N_DOM, NB, TERMS), 0, PARTNERS * SLOTS), jax.random.fold_in(streams_of[8], 1), 0, (PARTNERS * SLOTS) - 1).astype(jnp.int32),
        "remap_weight": draw_remap_weight(jax.random.fold_in(streams_of[10], 71), 0),
    }


def vertical(values, mix_rate):
    interface_flux = mix_rate[:, :, None, :] * (values[:, 1:] - values[:, :-1])
    zero_layer = jnp.zeros_like(values[:, :1])
    return values + jnp.concatenate([interface_flux, zero_layer], 1) - jnp.concatenate([zero_layer, interface_flux], 1)


def remap_device(device_item):
    received, slot_valid, source, weights_here = device_item
    chosen = received[source].astype(jnp.float32)
    source_valid = slot_valid[source]
    product = jnp.einsum("ntib,ntfb->ntfi", weights_here.astype(jnp.float32), chosen)
    numerator = jnp.sum(product * source_valid[:, :, None, None], axis=1)
    row_sums = jnp.sum(weights_here.astype(jnp.float32), axis=3)
    denominator = jnp.maximum(jnp.sum(row_sums * source_valid[:, :, None], axis=1), 1.0)
    return numerator / denominator[:, None, :]


def reference(column_state, vert_rate, hor_offsets, hor_coef, open_mask, couple_rate, send_index, live_slots, block_source, remap_weight):
    partners = 2 * RADIUS + 1
    mixed_state = vertical(column_state, vert_rate)
    surface = mixed_state[:, 0].reshape(2, F, N_DOM, COLS).transpose(0, 2, 1, 3)
    flat_index = send_index.reshape(2, N_DOM, 1, partners * SLOTS * BLKW)
    flat_index = jnp.broadcast_to(flat_index, (2, N_DOM, F, partners * SLOTS * BLKW))
    picked = jnp.take_along_axis(surface, flat_index, axis=3)
    sent_blocks = picked.reshape(2, N_DOM, F, partners, SLOTS, BLKW).transpose(0, 1, 3, 4, 2, 5).astype(jnp.bfloat16)
    swapped = sent_blocks[::-1]
    received = jnp.stack([jnp.roll(swapped[:, :, k], k - RADIUS, axis=1) for k in range(partners)], axis=2)
    received = received.reshape(2 * N_DOM, partners * SLOTS, F, BLKW)
    slot_valid = (jnp.arange(SLOTS, dtype=jnp.int32)[None, None, None, :] < live_slots[..., None]).astype(jnp.float32)
    slot_valid = slot_valid.reshape(2 * N_DOM, partners * SLOTS)
    blocks = lax.map(remap_device, (received, slot_valid, block_source.reshape(2 * N_DOM, NB, TERMS), remap_weight.reshape(2 * N_DOM, NB, TERMS, BLKW, BLKW)))
    forcing = blocks.reshape(2, N_DOM, NB, F, BLKW).transpose(0, 3, 1, 2, 4).reshape(2, F, N_DOM * COLS)
    open_float = open_mask.astype(jnp.float32)[:, None, :]
    new_top = mixed_state[:, 0] + couple_rate[:, :, None] * open_float * (forcing - mixed_state[:, 0])
    current = jnp.concatenate([new_top[:, None], mixed_state[:, 1:]], axis=1)
    positions = jnp.arange(NCOL, dtype=jnp.int32)
    for substep in range(NSUB):
        running = jnp.zeros_like(current)
        for j in range(6):
            neighbor = (positions[None, :] + hor_offsets[:, j]) % NCOL
            neighbor = jnp.broadcast_to(neighbor[:, None, None, :], current.shape)
            gathered = jnp.take_along_axis(current, neighbor, axis=3)
            running = running + hor_coef[:, j][:, None, None, :] * (gathered - current)
        current = current + running
    return current, forcing
```

```python
import jax
import jax.numpy as jnp
from jax import lax
from jax.experimental import pallas as pl
from jax.experimental.pallas import tpu as pltpu
from jax.sharding import PartitionSpec as P

F32, BF16 = jnp.float32, jnp.bfloat16
RIM = 512
NSUB = 4
TB = 256
WIN = TB + 2 * RIM
LANE = 128
NEVER = 8192.0
FIELDS, LEVELS, COLS = 16, 8, 2048
REST = (LEVELS - 1) * FIELDS
WIDE = COLS - RIM
VMEM_LIMIT = 56 * 2**20


def mix_kernel(state, rate, offs, coef, send, mix0, mixr, bulk, p0, p1, p2, p3, p4, tab_own, tab_low, tab_high):
    packed = (p0, p1, p2, p3, p4)
    for c in range(0, COLS, TB):
        here = slice(c, c + TB)
        v0 = state[0, :, here]
        mix0[:, here] = v0 + rate[0:1, here] * (state[1, :, here] - v0)
    for k in range(5):
        for j in range(4):
            for h in range(2):
                index = send[k, j : j + 1, h * LANE : (h + 1) * LANE]
                low = jnp.broadcast_to(index & (LANE - 1), (FIELDS, LANE))
                high = jnp.broadcast_to(lax.shift_right_logical(index, 7), (FIELDS, LANE))
                total = jnp.zeros((FIELDS, LANE), F32)
                for s in range(COLS // LANE):
                    got = jnp.take_along_axis(
                        mix0[:, s * LANE : (s + 1) * LANE], low, axis=1, mode="promise_in_bounds"
                    )
                    total = jnp.where(high == s, got, total)
                packed[k][j, :, h * LANE : (h + 1) * LANE] = total.astype(BF16)
    for c in range(0, COLS, TB):
        here = slice(c, c + TB)
        lane = lax.broadcasted_iota(jnp.int32, (1, TB), 1).astype(F32) + float(RIM)
        off = [offs[j : j + 1, here].astype(F32) for j in range(6)]
        val = [coef[j : j + 1, here] for j in range(6)]
        whole = jnp.zeros((1, TB), F32)
        rows_c, rows_p = [], []
        for j in range(6):
            merged = val[j]
            first = jnp.ones((1, TB), F32)
            for i in range(6):
                if i != j:
                    same = off[i] == off[j]
                    merged = merged + jnp.where(same, val[i], 0.0)
                    if i < j:
                        first = jnp.where(same, 0.0, first)
            merged = (merged * first).astype(BF16).astype(F32)
            whole = whole + merged
            rows_c.append(merged)
            rows_p.append(jnp.where(first > 0.5, off[j] + lane, NEVER))
        pad = [jnp.zeros((1, TB), F32)] * 3
        block = jnp.concatenate(rows_c + rows_p + [whole] + pad, axis=0)
        tab_own[:, here] = block
        if c < WIDE:
            tab_low[:, here] = block
        if c >= RIM:
            tab_high[:, c - RIM : c - RIM + TB] = block
    for c in range(0, COLS, TB):
        here = slice(c, c + TB)
        before = state[0, :, here]
        mid = state[1, :, here]
        flux = rate[0:1, here] * (mid - before)
        for l in range(1, LEVELS):
            if l < LEVELS - 1:
                after = state[l + 1, :, here]
                below = rate[l : l + 1, here] * (after - mid)
                new = mid + below - flux
                flux, mid = below, after
            else:
                new = mid - flux
            mixr[(l - 1) * FIELDS : l * FIELDS, here] = new
            bulk[(l - 1) * FIELDS : l * FIELDS, here] = new.astype(BF16)


def band_kernel(left, own, right, band, tab):
    b = pl.program_id(0)
    nl = WIDE // TB
    no = COLS // TB

    @pl.when(b < nl)
    def _():
        tab[...] = left[:, pl.ds(pl.multiple_of(b * TB, TB), TB)]

    @pl.when((b >= nl) & (b < nl + no))
    def _():
        tab[...] = own[:, pl.ds(pl.multiple_of((b - nl) * TB, TB), TB)]

    @pl.when(b >= nl + no)
    def _():
        tab[...] = right[:, pl.ds(pl.multiple_of((b - nl - no) * TB, TB), TB)]

    for half in range(TB // LANE):
        lanes = slice(half * LANE, (half + 1) * LANE)
        coefs = [jnp.broadcast_to(tab[j : j + 1, lanes], (16, LANE)).astype(BF16) for j in range(6)]
        first_row = half * LANE
        last_row = first_row + LANE + 2 * RIM
        if first_row:
            band[0, 0:first_row, lanes] = jnp.zeros((first_row, LANE), BF16)
        if last_row < WIN:
            band[0, last_row:WIN, lanes] = jnp.zeros((WIN - last_row, LANE), BF16)
        for base in range(first_row, last_row, LANE):
            rel = [
                jnp.broadcast_to(
                    jnp.clip(tab[6 + j : 7 + j, lanes] - float(base), -1.0, float(LANE)), (16, LANE)
                ).astype(BF16)
                for j in range(6)
            ]
            for r in range(0, LANE, 16):
                row = (lax.broadcasted_iota(jnp.int32, (16, LANE), 0).astype(F32) + float(r)).astype(BF16)
                total = jnp.zeros((16, LANE), BF16)
                for j in range(6):
                    total = jnp.where(rel[j] == row, coefs[j], total)
                band[0, base + r : base + r + 16, lanes] = total


def remap_kernel(live, source, r0, r1, r2, r3, r4, weights, mix0, mask, rate, forcing, top, top_half, got):
    for k, piece in enumerate((r0, r1, r2, r3, r4)):
        got[4 * k : 4 * k + 4] = piece[...]
    ones = jnp.ones((16, TB), BF16)
    for n in range(COLS // TB):
        here = slice(n * TB, (n + 1) * TB)
        num = jnp.zeros((FIELDS, TB), F32)
        den = jnp.zeros((1, TB), F32)
        for m in range(2):
            q = source[n, m]
            valid = jnp.where((q & 3) < live[lax.shift_right_logical(q, 2)], 1.0, 0.0).astype(F32)
            rows = jnp.concatenate([got[q], ones], axis=0)
            both = lax.dot_general(
                rows, weights[n, m], (((1,), (1,)), ((), ())), preferred_element_type=F32
            )
            num = num + valid * both[0:FIELDS]
            den = den + valid * both[FIELDS : FIELDS + 1]
        value = num / jnp.maximum(den, 1.0)
        forcing[:, here] = value
        old = mix0[:, here]
        new = old + rate[...] * mask[0:1, here].astype(F32) * (value - old)
        top[:, here] = new
        top_half[:, here] = new.astype(BF16)


def diffuse_kernel(
    band, mixr, bulk, bulk_l, bulk_r, top, top_half, top_l, top_r, tab_l, tab_o, tab_r,
    out, bands, xa, xb, st, whole, sems, band_sems,
):
    nb = band.shape[0]
    copies = [
        (bulk_l, xa.at[FIELDS:, 0:COLS]),
        (bulk, xa.at[FIELDS:, COLS : 2 * COLS]),
        (bulk_r, xa.at[FIELDS:, 2 * COLS : 3 * COLS]),
        (top_l, xa.at[0:FIELDS, 0:COLS]),
        (top_half, xa.at[0:FIELDS, COLS : 2 * COLS]),
        (top_r, xa.at[0:FIELDS, 2 * COLS : 3 * COLS]),
        (mixr, st.at[FIELDS:, WIDE : WIDE + COLS]),
        (top, st.at[0:FIELDS, WIDE : WIDE + COLS]),
    ]
    copies = [pltpu.make_async_copy(a, b, sems.at[i]) for i, (a, b) in enumerate(copies)]
    for c in copies:
        c.start()
    fetch = [pltpu.make_async_copy(band.at[i], bands.at[i], band_sems.at[i]) for i in range(nb)]
    for c in fetch:
        c.start()
    whole[:, 0:WIDE] = 1.0 - tab_l[12:13]
    whole[:, WIDE : WIDE + COLS] = 1.0 - tab_o[12:13]
    whole[:, WIDE + COLS :] = 1.0 - tab_r[12:13]
    for c in copies:
        c.wait()
    bufs = (xa, xb)
    edge = WIDE // TB
    for step in range(NSUB):
        src, dst = bufs[step % 2], bufs[(step + 1) % 2]
        skip = step * (RIM // TB)
        for b in range(skip, nb - skip):
            if step == 0:
                fetch[b].wait()
            at = slice(b * TB, (b + 1) * TB)
            here = slice(RIM + b * TB, RIM + (b + 1) * TB)
            acc = jnp.dot(src[:, b * TB : b * TB + WIN], bands[b], preferred_element_type=F32)
            if step == 0 and (b < edge or b >= nb - edge):
                old = src[:, here].astype(F32)
            else:
                old = st[:, at]
            new = old * whole[:, at] + acc
            if step < NSUB - 1:
                st[:, at] = new
                dst[:, here] = new.astype(BF16)
            else:
                out[:, (b - edge) * TB : (b - edge + 1) * TB] = new


def neighbour(value, flip, apart):
    size = (lax.axis_size("comp"), lax.axis_size("dom"))
    pairs = [
        (s * size[1] + d, (s ^ flip) * size[1] + (d + apart) % size[1])
        for s in range(size[0])
        for d in range(size[1])
    ]
    return lax.ppermute(value, ("comp", "dom"), pairs)


def spec(n):
    return [pl.BlockSpec(memory_space=pltpu.VMEM)] * n


ANYWHERE = pl.BlockSpec(memory_space=pl.ANY)
SCALARS = pl.BlockSpec(memory_space=pltpu.SMEM)


def params(**more):
    return pltpu.CompilerParams(vmem_limit_bytes=VMEM_LIMIT, **more)


def shards(
    column_state, vert_rate, hor_offsets, hor_coef, open_mask, couple_rate, send_index, live_slots, block_source,
    remap_weight,
):
    shape = jax.ShapeDtypeStruct
    block = shape((4, FIELDS, TB), BF16)
    mix0, mixr, bulk, p0, p1, p2, p3, p4, tab_own, tab_low, tab_high = pl.pallas_call(
        mix_kernel,
        out_shape=[
            shape((FIELDS, COLS), F32),
            shape((REST, COLS), F32),
            shape((REST, COLS), BF16),
            block, block, block, block, block,
            shape((16, COLS), F32),
            shape((16, WIDE), F32),
            shape((16, WIDE), F32),
        ],
        in_specs=spec(5),
        out_specs=spec(11),
        compiler_params=params(),
        name="mix",
    )(column_state[0], vert_rate[0], hor_offsets[0], hor_coef[0], send_index[0, 0])

    tab_left = neighbour(tab_high, 0, 1)
    tab_right = neighbour(tab_low, 0, -1)
    received = [neighbour(p, 1, k - 2) for k, p in enumerate((p0, p1, p2, p3, p4))]
    bulk_left = neighbour(bulk, 0, 1)
    bulk_right = neighbour(bulk, 0, -1)

    nb = (COLS + 2 * WIDE) // TB
    band = pl.pallas_call(
        band_kernel,
        grid=(nb,),
        out_shape=shape((nb, WIN, TB), BF16),
        in_specs=spec(3),
        out_specs=pl.BlockSpec((1, WIN, TB), lambda b: (b, 0, 0)),
        scratch_shapes=[pltpu.VMEM((16, TB), F32)],
        compiler_params=params(),
        cost_estimate=pl.CostEstimate(flops=0, bytes_accessed=30_000_000, transcendentals=0),
        name="band",
    )(tab_left, tab_own, tab_right)

    forcing, top, top_half = pl.pallas_call(
        remap_kernel,
        out_shape=[shape((FIELDS, COLS), F32), shape((FIELDS, COLS), F32), shape((FIELDS, COLS), BF16)],
        in_specs=[SCALARS, SCALARS] + spec(9),
        out_specs=spec(3),
        scratch_shapes=[pltpu.VMEM((20, FIELDS, TB), BF16)],
        compiler_params=params(),
        name="remap",
    )(live_slots[0, 0], block_source[0, 0], *received, remap_weight[0, 0], mix0, open_mask, couple_rate[0][:, None])

    top_left = neighbour(top_half, 0, 1)
    top_right = neighbour(top_half, 0, -1)

    state = pl.pallas_call(
        diffuse_kernel,
        out_shape=shape((LEVELS * FIELDS, COLS), F32),
        in_specs=[ANYWHERE] * 9 + spec(3),
        out_specs=pl.BlockSpec(memory_space=pltpu.VMEM),
        scratch_shapes=[
            pltpu.VMEM((nb, WIN, TB), BF16),
            pltpu.VMEM((LEVELS * FIELDS, 3 * COLS), BF16),
            pltpu.VMEM((LEVELS * FIELDS, 3 * COLS), BF16),
            pltpu.VMEM((LEVELS * FIELDS, COLS + 2 * WIDE), F32),
            pltpu.VMEM((1, COLS + 2 * WIDE), F32),
            pltpu.SemaphoreType.DMA((8,)),
            pltpu.SemaphoreType.DMA((nb,)),
        ],
        compiler_params=params(),
        name="diffuse",
    )(band, mixr, bulk, bulk_left, bulk_right, top, top_half, top_left, top_right, tab_left, tab_own, tab_right)
    return state.reshape(1, LEVELS, FIELDS, COLS), forcing[None]


def solution(mesh):
    placed = (
        P("comp", None, None, "dom"),
        P("comp", None, "dom"),
        P("comp", None, "dom"),
        P("comp", None, "dom"),
        P("comp", "dom"),
        P("comp", None),
        P("comp", "dom", None, None, None),
        P("comp", "dom", None),
        P("comp", "dom", None, None),
        P("comp", "dom", None, None, None, None),
    )
    return jax.shard_map(
        shards,
        mesh=mesh,
        in_specs=placed,
        out_specs=(P("comp", None, None, "dom"), P("comp", None, "dom")),
        check_vma=False,
    )
```

```python
import jax
import jax.numpy as jnp
from jax import lax
from jax.experimental import pallas as pl
from jax.experimental.pallas import tpu as pltpu
from jax.sharding import PartitionSpec as P

F32, BF16 = jnp.float32, jnp.bfloat16
RIM = 512
NSUB = 4
TB = 256
WIN = TB + 2 * RIM
LANE = 128
NEVER = 64.0
FIELDS, LEVELS, COLS = 16, 8, 2048
REST = (LEVELS - 1) * FIELDS
WIDE = COLS - RIM
TABLE = 32


def pick_kernel(state, rate, send, mix0, p0, p1, p2, p3, p4):
    packed = (p0, p1, p2, p3, p4)
    for c in range(0, COLS, TB):
        here = slice(c, c + TB)
        v0 = state[0, 0, :, here]
        mix0[:, here] = v0 + rate[0, :, here] * (state[0, 1, :, here] - v0)
    for k in range(5):
        for j in range(4):
            for h in range(2):
                index = send[k, j : j + 1, h * LANE : (h + 1) * LANE]
                low = jnp.broadcast_to(index & (LANE - 1), (FIELDS, LANE))
                high = jnp.broadcast_to(lax.shift_right_logical(index, 7), (FIELDS, LANE))
                total = jnp.zeros((FIELDS, LANE), F32)
                for s in range(COLS // LANE):
                    got = jnp.take_along_axis(
                        mix0[:, s * LANE : (s + 1) * LANE], low, axis=1, mode="promise_in_bounds"
                    )
                    total = jnp.where(high == s, got, total)
                packed[k][j, :, h * LANE : (h + 1) * LANE] = total.astype(BF16)


def rest_kernel(state, rate, offs, coef, after, mixr, bulk):
    del after
    for c in range(0, COLS, TB):
        here = slice(c, c + TB)
        before = state[0, 0, :, here]
        mid = state[0, 1, :, here]
        flux = rate[0, :, here] * (mid - before)
        for l in range(1, LEVELS):
            if l < LEVELS - 1:
                after = state[0, l + 1, :, here]
                below = rate[l, :, here] * (after - mid)
                new = mid + below - flux
                flux, mid = below, after
            else:
                new = mid - flux
            mixr[(l - 1) * FIELDS : l * FIELDS, here] = new
            bulk[(l - 1) * FIELDS : l * FIELDS, here] = new.astype(BF16)
        lane = lax.broadcasted_iota(jnp.int32, (1, TB), 1) + RIM
        off = [offs[j, :, here] for j in range(6)]
        val = [coef[j, :, here] for j in range(6)]
        zero = jnp.zeros((1, TB), F32)
        rows_c, rows_h, rows_l = [], [], []
        for j in range(6):
            merged = val[j]
            repeated = zero
            for i in range(6):
                if i != j:
                    same = off[i] == off[j]
                    merged = merged + jnp.where(same, val[i], 0.0)
                    if i < j:
                        repeated = jnp.where(same, 1.0, repeated)
            place = off[j] + lane
            rows_c.append(jnp.where(repeated > 0.5, 0.0, merged))
            rows_h.append(jnp.where(repeated > 0.5, NEVER, lax.shift_right_logical(place, 7).astype(F32)))
            rows_l.append((place & (LANE - 1)).astype(F32))
        block = jnp.concatenate(rows_c + [zero] * 2 + rows_h + [zero] * 2 + rows_l + [zero] * 10, axis=0)
        bulk[REST : REST + TABLE, here] = block.astype(BF16)


def build_bands(tab, rel, band, first, count, source):
    columns = count * TB
    tab[0:8, 0:columns] = source[0:16, 0:columns].astype(F32)[0:8]
    high = source[0:16, 0:columns].astype(F32)[8:16]
    low = source[16:32, 0:columns].astype(F32)[0:8]
    tab[8:16, 0:columns] = high * float(LANE) + low
    rows = [
        (lax.broadcasted_iota(jnp.int32, (16, LANE), 0) + r).astype(F32).astype(BF16) for r in range(0, LANE, 16)
    ]

    @pl.loop(0, count)
    def _(b):
        for half in range(TB // LANE):
            start = pl.multiple_of(b * TB + half * LANE, LANE)
            lanes = slice(half * LANE, (half + 1) * LANE)
            coefs = [
                jnp.broadcast_to(tab[j : j + 1, pl.ds(start, LANE)], (16, LANE)).astype(BF16) for j in range(6)
            ]
            first_row = half * LANE
            last_row = first_row + LANE + 2 * RIM
            if first_row:
                band[first + b, 0:first_row, lanes] = jnp.zeros((first_row, LANE), BF16)
            if last_row < WIN:
                band[first + b, last_row:WIN, lanes] = jnp.zeros((WIN - last_row, LANE), BF16)
            for base in range(first_row, last_row, LANE):
                slot = 8 * (half * (WIN // LANE) + base // LANE)
                rel[slot : slot + 8, :] = tab[8:16, pl.ds(start, LANE)] - float(base)
                there = [
                    jnp.broadcast_to(rel[slot + j : slot + j + 1, :], (16, LANE)).astype(BF16) for j in range(6)
                ]
                for r in range(0, LANE, 16):
                    total = jnp.zeros((16, LANE), BF16)
                    for j in range(6):
                        total = jnp.where(there[j] == rows[r // 16], coefs[j], total)
                    band[first + b, base + r : base + r + 16, lanes] = total


def own_band_kernel(bulk, band, raw, tab, rel, sem):
    copy = pltpu.make_async_copy(bulk.at[REST : REST + TABLE], raw, sem)
    copy.start()
    copy.wait()
    build_bands(tab, rel, band, 0, COLS // TB, raw)


def side_band_kernel(bulk_l, bulk, bulk_r, band, wide, keep, raw_l, raw_o, raw_r, tab, rel, sems):
    tables = [
        pltpu.make_async_copy(bulk_l.at[REST : REST + TABLE, RIM:COLS], raw_l, sems.at[0]),
        pltpu.make_async_copy(bulk.at[REST : REST + TABLE], raw_o, sems.at[1]),
        pltpu.make_async_copy(bulk_r.at[REST : REST + TABLE, 0:WIDE], raw_r, sems.at[2]),
    ]
    fields = [
        pltpu.make_async_copy(piece.at[0:REST], wide.at[:, i * COLS : (i + 1) * COLS], sems.at[3 + i])
        for i, piece in enumerate((bulk_l, bulk, bulk_r))
    ]
    for c in tables + fields:
        c.start()
    for c in tables:
        c.wait()
    at = 0
    for raw, columns in ((raw_l, WIDE), (raw_o, COLS), (raw_r, WIDE)):
        coefs = raw[0:16, :].astype(F32)[0:8]
        keep[:, at : at + columns] = 1.0 - jnp.sum(coefs, axis=0, keepdims=True)
        at += columns
    build_bands(tab, rel, band, 0, WIDE // TB, raw_l)
    build_bands(tab, rel, band, WIDE // TB, WIDE // TB, raw_r)
    for c in fields:
        c.wait()


def remap_kernel(live, source, r0, r1, r2, r3, r4, weights, mix0, mask, rate, after, forcing, top, top_half, got):
    del after
    for k, piece in enumerate((r0, r1, r2, r3, r4)):
        got[4 * k : 4 * k + 4] = piece[...]
    ones = jnp.ones((16, TB), BF16)
    eye = lax.broadcasted_iota(jnp.int32, (FIELDS, FIELDS), 0) == lax.broadcasted_iota(
        jnp.int32, (FIELDS, FIELDS), 1
    )
    rate_column = jnp.sum(
        jnp.where(eye, jnp.broadcast_to(rate[...], (FIELDS, FIELDS)), 0.0), axis=1, keepdims=True
    )
    for n in range(COLS // TB):
        here = slice(n * TB, (n + 1) * TB)
        num = jnp.zeros((FIELDS, TB), F32)
        den = jnp.zeros((1, TB), F32)
        for m in range(2):
            q = source[m, n]
            valid = jnp.where((q & 3) < live[0, lax.shift_right_logical(q, 2)], 1.0, 0.0).astype(F32)
            rows = jnp.concatenate([got[q], ones], axis=0)
            both = lax.dot_general(
                rows, weights[n, m], (((1,), (1,)), ((), ())), preferred_element_type=F32
            )
            num = num + valid * both[0:FIELDS]
            den = den + valid * both[FIELDS : FIELDS + 1]
        value = num / jnp.maximum(den, 1.0)
        forcing[:, here] = value
        old = mix0[:, here]
        new = old + rate_column * mask[0:1, here].astype(F32) * (value - old)
        top[:, here] = new
        top_half[:, here] = new.astype(BF16)


def diffuse_kernel(
    band_own, band_side, wide, keep, mixr, top, top_half, top_l, top_r, out, xt, xa, xb, st,
):
    xt[:, 0:COLS] = top_l[...]
    xt[:, COLS : 2 * COLS] = top_half[...]
    xt[:, 2 * COLS : 3 * COLS] = top_r[...]
    edge = WIDE // TB
    own = COLS // TB
    nb = own + 2 * edge
    bufs = (xa, xb)
    for step in range(NSUB):
        src, dst = bufs[(step + 1) % 2], bufs[step % 2]
        skip = step * (RIM // TB)
        for b in range(skip, nb - skip):
            at = slice(b * TB, (b + 1) * TB)
            here = slice(RIM + b * TB, RIM + (b + 1) * TB)
            window = slice(b * TB, b * TB + WIN)
            inside = edge <= b < edge + own
            mine = slice((b - edge) * TB, (b - edge + 1) * TB)
            if inside:
                matrix = band_own[b - edge]
            else:
                matrix = band_side[b if b < edge else b - own]
            if step == 0:
                rows = jnp.concatenate([xt[:, window], wide[:, window]], axis=0)
                if inside:
                    old = jnp.concatenate([top[:, mine], mixr[:, mine]], axis=0)
                else:
                    old = jnp.concatenate([xt[:, here], wide[:, here]], axis=0).astype(F32)
            else:
                rows = src[:, window]
                old = st[:, at]
            new = old * keep[:, at] + jnp.dot(rows, matrix, preferred_element_type=F32)
            if step < NSUB - 1:
                st[:, at] = new
                dst[:, here] = new.astype(BF16)
            else:
                out[:, mine] = new


def neighbour(value, flip, apart):
    size = (lax.axis_size("comp"), lax.axis_size("dom"))
    pairs = [
        (s * size[1] + d, (s ^ flip) * size[1] + (d + apart) % size[1])
        for s in range(size[0])
        for d in range(size[1])
    ]
    return lax.ppermute(value, ("comp", "dom"), pairs)


def spec(n):
    return [pl.BlockSpec(memory_space=pltpu.VMEM)] * n


ANYWHERE = pl.BlockSpec(memory_space=pl.ANY)
SCALARS = pl.BlockSpec(memory_space=pltpu.SMEM)


def params(mib):
    return pltpu.CompilerParams(vmem_limit_bytes=mib * 2**20)


def cost(us):
    return pl.CostEstimate(flops=0, bytes_accessed=us * 3_000_000, transcendentals=0)


def shards(
    column_state, vert_rate, hor_offsets, hor_coef, open_mask, couple_rate, send_index, live_slots, block_source,
    remap_weight,
):
    shape = jax.ShapeDtypeStruct
    block = shape((4, FIELDS, TB), BF16)
    rate = vert_rate.transpose(1, 0, 2)
    mix0, p0, p1, p2, p3, p4 = pl.pallas_call(
        pick_kernel,
        grid=(1,),
        out_shape=[shape((FIELDS, COLS), F32)] + [block] * 5,
        in_specs=[
            pl.BlockSpec((1, 2, FIELDS, COLS), lambda i: (0, 0, 0, 0)),
            pl.BlockSpec((1, 1, COLS), lambda i: (0, 0, 0)),
        ]
        + spec(1),
        out_specs=spec(6),
        compiler_params=params(8),
        cost_estimate=cost(2),
        name="pick",
    )(column_state, rate, send_index[0, 0])
    received = [neighbour(p, 1, k - 2) for k, p in enumerate((p0, p1, p2, p3, p4))]

    mixr, bulk = pl.pallas_call(
        rest_kernel,
        out_shape=[shape((REST, COLS), F32), shape((REST + TABLE, COLS), BF16)],
        in_specs=spec(4) + [ANYWHERE],
        out_specs=spec(2),
        compiler_params=params(8),
        cost_estimate=cost(2),
        name="rest",
    )(column_state, rate, hor_offsets.transpose(1, 0, 2), hor_coef.transpose(1, 0, 2), p4)
    bulk_left = neighbour(bulk, 0, 1)
    bulk_right = neighbour(bulk, 0, -1)

    raw = pltpu.VMEM((TABLE, COLS), BF16)
    raw_side = pltpu.VMEM((TABLE, WIDE), BF16)
    tab = pltpu.VMEM((16, COLS), F32)
    rel = pltpu.VMEM((16 * (WIN // LANE), LANE), F32)
    band_own = pl.pallas_call(
        own_band_kernel,
        out_shape=shape((COLS // TB, WIN, TB), BF16),
        in_specs=[ANYWHERE],
        out_specs=pl.BlockSpec(memory_space=pltpu.VMEM),
        scratch_shapes=[raw, tab, rel, pltpu.SemaphoreType.DMA],
        compiler_params=params(8),
        cost_estimate=cost(3),
        name="own_band",
    )(bulk)

    forcing, top, top_half = pl.pallas_call(
        remap_kernel,
        out_shape=[shape((FIELDS, COLS), F32), shape((FIELDS, COLS), F32), shape((FIELDS, COLS), BF16)],
        in_specs=[SCALARS, SCALARS] + spec(9) + [ANYWHERE],
        out_specs=spec(3),
        scratch_shapes=[pltpu.VMEM((20, FIELDS, TB), BF16)],
        compiler_params=params(8),
        cost_estimate=cost(2),
        name="remap",
    )(live_slots[0], block_source[0, 0].T, *received, remap_weight[0, 0], mix0, open_mask, couple_rate, band_own)
    top_left = neighbour(top_half, 0, 1)
    top_right = neighbour(top_half, 0, -1)

    band_side, wide, keep = pl.pallas_call(
        side_band_kernel,
        out_shape=[
            shape((2 * WIDE // TB, WIN, TB), BF16),
            shape((REST, 3 * COLS), BF16),
            shape((1, COLS + 2 * WIDE), F32),
        ],
        in_specs=[ANYWHERE] * 3,
        out_specs=spec(3),
        scratch_shapes=[raw_side, raw, raw_side, tab, rel, pltpu.SemaphoreType.DMA((6,))],
        compiler_params=params(8),
        cost_estimate=cost(4),
        name="side_band",
    )(bulk_left, bulk, bulk_right)

    half = pltpu.VMEM((LEVELS * FIELDS, 3 * COLS), BF16)
    state = pl.pallas_call(
        diffuse_kernel,
        out_shape=shape((LEVELS * FIELDS, COLS), F32),
        in_specs=spec(9),
        out_specs=pl.BlockSpec(memory_space=pltpu.VMEM),
        scratch_shapes=[
            pltpu.VMEM((FIELDS, 3 * COLS), BF16),
            half,
            half,
            pltpu.VMEM((LEVELS * FIELDS, COLS + 2 * WIDE), F32),
        ],
        compiler_params=params(16),
        cost_estimate=cost(6),
        name="diffuse",
    )(band_own, band_side, wide, keep, mixr, top, top_half, top_left, top_right)
    return state.reshape(1, LEVELS, FIELDS, COLS), forcing[None]


def solution(mesh):
    placed = (
        P("comp", None, None, "dom"),
        P("comp", None, "dom"),
        P("comp", None, "dom"),
        P("comp", None, "dom"),
        P("comp", "dom"),
        P("comp", None),
        P("comp", "dom", None, None, None),
        P("comp", "dom", None),
        P("comp", "dom", None, None),
        P("comp", "dom", None, None, None, None),
    )
    return jax.shard_map(
        shards,
        mesh=mesh,
        in_specs=placed,
        out_specs=(P("comp", None, None, "dom"), P("comp", None, "dom")),
        check_vma=False,
    )
```

```python
import jax
import jax.numpy as jnp
from jax import lax
from jax.experimental import pallas as pl
from jax.experimental.pallas import tpu as pltpu
from jax.sharding import PartitionSpec as P

F32, BF16 = jnp.float32, jnp.bfloat16
RIM = 512
NSUB = 4
TB = 256
WIN = TB + 2 * RIM
LANE = 128
NEVER = 64.0
FIELDS, LEVELS, COLS = 16, 8, 2048
REST = (LEVELS - 1) * FIELDS
WIDE = COLS - RIM
PICK_MIB = 63
PAY = 4 + 2 * WIDE // TB


def mix_kernel(
    state_hbm, rate_hbm, send_hbm, offs_hbm, coef_hbm, mask_hbm, couple_hbm, packed, mix0, mixr, bulk, tabs, gate,
    state, rate, send, offs, coef, mask, couple, sems,
):
    pairs = (
        (state_hbm.at[0, 0:2], state.at[0:2]),
        (rate_hbm, rate),
        (send_hbm, send),
        (offs_hbm, offs),
        (coef_hbm, coef),
        (mask_hbm, mask),
        (couple_hbm, couple),
        (state_hbm.at[0, 2:LEVELS], state.at[2:LEVELS]),
    )
    copies = [pltpu.make_async_copy(a, b, sems.at[i]) for i, (a, b) in enumerate(pairs)]
    for copy in copies:
        copy.start()
    for copy in copies[:3]:
        copy.wait()
    for c in range(0, COLS, TB):
        here = slice(c, c + TB)
        v0 = state[0, :, here]
        mix0[:, here] = v0 + rate[0, :, here] * (state[1, :, here] - v0)
    for k in range(5):
        for j in range(4):
            for h in range(2):
                index = send[k, j : j + 1, h * LANE : (h + 1) * LANE]
                low = jnp.broadcast_to(index & (LANE - 1), (FIELDS, LANE))
                high = jnp.broadcast_to(lax.shift_right_logical(index, 7), (FIELDS, LANE))
                total = jnp.zeros((FIELDS, LANE), F32)
                for p in range(COLS // LANE):
                    got = jnp.take_along_axis(
                        mix0[:, p * LANE : (p + 1) * LANE], low, axis=1, mode="promise_in_bounds"
                    )
                    total = jnp.where(high == p, got, total)
                packed[k, j, :, h * LANE : (h + 1) * LANE] = total.astype(BF16)
    for copy in copies[3:]:
        copy.wait()
    eye = lax.broadcasted_iota(jnp.int32, (FIELDS, FIELDS), 0) == lax.broadcasted_iota(
        jnp.int32, (FIELDS, FIELDS), 1
    )
    couple_column = jnp.sum(
        jnp.where(eye, jnp.broadcast_to(couple[...], (FIELDS, FIELDS)), 0.0), axis=1, keepdims=True
    )
    for n in range(COLS // TB):
        here = slice(n * TB, (n + 1) * TB)
        gate[:, here] = couple_column * mask[0:1, here].astype(F32)
        before = state[0, :, here]
        mid = state[1, :, here]
        flux = rate[0, :, here] * (mid - before)
        for l in range(1, LEVELS):
            if l < LEVELS - 1:
                after_mid = state[l + 1, :, here]
                below = rate[l, :, here] * (after_mid - mid)
                new = mid + below - flux
                flux, mid = below, after_mid
            else:
                new = mid - flux
            mixr[(l - 1) * FIELDS : l * FIELDS, here] = new
            bulk[(l - 1) * FIELDS : l * FIELDS, here] = new.astype(BF16)
        lane = lax.broadcasted_iota(jnp.int32, (1, TB), 1) + RIM
        off = [offs[j, :, here] for j in range(6)]
        val = [coef[j, :, here] for j in range(6)]
        zero = jnp.zeros((1, TB), F32)
        rows_c, rows_h, rows_l = [], [], []
        for j in range(6):
            merged = val[j]
            repeated = zero
            for i in range(6):
                if i != j:
                    same = off[i] == off[j]
                    merged = merged + jnp.where(same, val[i], 0.0)
                    if i < j:
                        repeated = jnp.where(same, 1.0, repeated)
            place = off[j] + lane
            rows_c.append(jnp.where(repeated > 0.5, 0.0, merged))
            rows_h.append(jnp.where(repeated > 0.5, NEVER, lax.shift_right_logical(place, 7).astype(F32)))
            rows_l.append((place & (LANE - 1)).astype(F32))
        tabs[2 * n] = jnp.concatenate(rows_c + [zero] * 2 + rows_h + [zero] * 2, axis=0).astype(BF16)
        tabs[2 * n + 1] = jnp.concatenate(rows_l + [zero] * 10, axis=0).astype(BF16)


def parities():
    d = lax.axis_index("dom")
    return (d & 1) == 0, (d & 2) == 0


def stage_kernel(swapped, tabs, e1, o1, e2, o2, kept):
    near, far = parities()
    e1[0:4] = swapped[jnp.where(near, 3, 1)]
    e1[4:PAY] = tabs[pl.ds(jnp.where(near, 2 * COLS // TB - (PAY - 4), 0), PAY - 4)]
    o1[0:4] = swapped[jnp.where(near, 1, 3)]
    o1[4:PAY] = tabs[pl.ds(jnp.where(near, 0, 2 * COLS // TB - (PAY - 4)), PAY - 4)]
    kept[...] = tabs[...]
    e2[...] = swapped[jnp.where(far, 4, 0)]
    o2[...] = swapped[jnp.where(far, 0, 4)]


def build_bands(tab, rel, band, into, count, tabs, start):
    rows = [
        (lax.broadcasted_iota(jnp.int32, (16, LANE), 0) + r).astype(F32).astype(BF16) for r in range(0, LANE, 16)
    ]

    @pl.loop(0, count)
    def _(b):
        first = tabs[start + 2 * b].astype(F32)
        second = tabs[start + 2 * b + 1].astype(F32)
        tab[0:8] = first[0:8]
        tab[8:16] = first[8:16] * float(LANE) + second[0:8]
        for half in range(TB // LANE):
            lanes = slice(half * LANE, (half + 1) * LANE)
            coefs = [jnp.broadcast_to(tab[j : j + 1, lanes], (16, LANE)).astype(BF16) for j in range(6)]
            first_row = half * LANE
            last_row = first_row + LANE + 2 * RIM
            if first_row:
                band[into + b, 0:first_row, lanes] = jnp.zeros((first_row, LANE), BF16)
            if last_row < WIN:
                band[into + b, last_row:WIN, lanes] = jnp.zeros((WIN - last_row, LANE), BF16)
            for base in range(first_row, last_row, LANE):
                slot = 8 * (half * (WIN // LANE) + base // LANE)
                rel[slot : slot + 8, :] = tab[8:16, lanes] - float(base)
                there = [
                    jnp.broadcast_to(rel[slot + j : slot + j + 1, :], (16, LANE)).astype(BF16) for j in range(6)
                ]
                for r in range(0, LANE, 16):
                    total = jnp.zeros((16, LANE), BF16)
                    for j in range(6):
                        total = jnp.where(there[j] == rows[r // 16], coefs[j], total)
                    band[into + b, base + r : base + r + 16, lanes] = total


def own_band_kernel(tabs, after, band, tab, rel):
    del after
    build_bands(tab, rel, band, 0, COLS // TB, tabs, 0)


def side_band_kernel(e1, tabs, o1, after, band, keep, tab, rel):
    del after
    near, _ = parities()
    side = WIDE // TB
    places = (
        (e1, 4, side, jnp.where(near, WIDE + COLS, 0)),
        (tabs, 0, COLS // TB, WIDE),
        (o1, 4, side, jnp.where(near, 0, WIDE + COLS)),
    )
    for ref, start, count, base in places:
        for b in range(count):
            coefs = ref[start + 2 * b].astype(F32)[0:8]
            at = base + b * TB
            at = at if isinstance(at, int) else pl.multiple_of(at, TB)
            keep[:, pl.ds(at, TB)] = 1.0 - jnp.sum(coefs, axis=0, keepdims=True)
    build_bands(tab, rel, band, jnp.where(near, side, 0), side, e1, 4)
    build_bands(tab, rel, band, jnp.where(near, 0, side), side, o1, 4)


def remap_kernel(live, source, e1, o1, e2, o2, swapped, weights, mix0, gate, after, forcing, top, top_half, got):
    del after
    near, far = parities()
    got[pl.ds(jnp.where(far, 0, 16), 4)] = e2[...]
    got[pl.ds(jnp.where(near, 4, 12), 4)] = e1[0:4]
    got[8:12] = swapped[2]
    got[pl.ds(jnp.where(near, 12, 4), 4)] = o1[0:4]
    got[pl.ds(jnp.where(far, 16, 0), 4)] = o2[...]
    ones = jnp.ones((16, TB), BF16)
    for n in range(COLS // TB):
        here = slice(n * TB, (n + 1) * TB)
        num = jnp.zeros((FIELDS, TB), F32)
        den = jnp.zeros((1, TB), F32)
        for m in range(2):
            q = source[m, n]
            valid = jnp.where((q & 3) < live[0, lax.shift_right_logical(q, 2)], 1.0, 0.0).astype(F32)
            rows = jnp.concatenate([got[q], ones], axis=0)
            both = lax.dot_general(
                rows, weights[n, m], (((1,), (1,)), ((), ())), preferred_element_type=F32
            )
            num = num + valid * both[0:FIELDS]
            den = den + valid * both[FIELDS : FIELDS + 1]
        value = num / jnp.maximum(den, 1.0)
        forcing[:, here] = value
        old = mix0[:, here]
        new = old + gate[:, here] * (value - old)
        top[:, here] = new
        top_half[:, here] = new.astype(BF16)


def columns_of(parts, start, size):
    pieces = []
    while size:
        which, at = divmod(start, COLS)
        step = min(size, COLS - at)
        pieces.append(parts[which][:, at : at + step])
        start, size = start + step, size - step
    return pieces[0] if len(pieces) == 1 else jnp.concatenate(pieces, axis=1)


def diffuse_kernel(
    band_own, band_side, keep, mixr, bulk_e, bulk, bulk_o, top, top_e, top_half, top_o, out, xa, xb, st,
):
    edge = WIDE // TB
    own = COLS // TB
    nb = own + 2 * edge
    bufs = (xa, xb)

    def matrix(b):
        if edge <= b < edge + own:
            return band_own[b - edge]
        return band_side[b if b < edge else b - own]

    def first_step(tops, rests):
        for b in range(nb):
            at = slice(b * TB, (b + 1) * TB)
            mine = slice((b - edge) * TB, (b - edge + 1) * TB)
            rows = jnp.concatenate([columns_of(tops, b * TB, WIN), columns_of(rests, b * TB, WIN)], axis=0)
            if edge <= b < edge + own:
                old = jnp.concatenate([top[:, mine], mixr[:, mine]], axis=0)
            else:
                start = RIM + b * TB
                old = jnp.concatenate([columns_of(tops, start, TB), columns_of(rests, start, TB)], axis=0).astype(F32)
            new = old * keep[:, at] + jnp.dot(rows, matrix(b), preferred_element_type=F32)
            st[:, at] = new
            xa[:, at] = new.astype(BF16)

    near, _ = parities()

    @pl.when(near)
    def _():
        first_step((top_o, top_half, top_e), (bulk_o, bulk, bulk_e))

    @pl.when(jnp.logical_not(near))
    def _():
        first_step((top_e, top_half, top_o), (bulk_e, bulk, bulk_o))

    for step in range(1, NSUB):
        src, dst = bufs[(step + 1) % 2], bufs[step % 2]
        skip = step * (RIM // TB)
        for b in range(skip, nb - skip):
            at = slice(b * TB, (b + 1) * TB)
            rows = src[:, b * TB - RIM : b * TB - RIM + WIN]
            new = st[:, at] * keep[:, at] + jnp.dot(rows, matrix(b), preferred_element_type=F32)
            if step < NSUB - 1:
                st[:, at] = new
                dst[:, at] = new.astype(BF16)
            else:
                out[:, (b - edge) * TB : (b - edge + 1) * TB] = new


def crossed(value):
    size = (lax.axis_size("comp"), lax.axis_size("dom"))
    pairs = [(s * size[1] + d, (1 - s) * size[1] + d) for s in range(size[0]) for d in range(size[1])]
    return lax.ppermute(value, ("comp", "dom"), pairs)


def paired(value, apart, odd):
    count = lax.axis_size("dom")
    pairs = [(d, (d + (apart if bool(d & apart) == odd else -apart)) % count) for d in range(count)]
    return lax.ppermute(value, "dom", pairs)


def spec(n):
    return [pl.BlockSpec(memory_space=pltpu.VMEM)] * n


ANYWHERE = pl.BlockSpec(memory_space=pl.ANY)
SCALARS = pl.BlockSpec(memory_space=pltpu.SMEM)


def params(mib):
    return pltpu.CompilerParams(vmem_limit_bytes=mib * 2**20)


def cost(us):
    return pl.CostEstimate(flops=0, bytes_accessed=us * 3_000_000, transcendentals=0)


def shards(
    column_state, vert_rate, hor_offsets, hor_coef, open_mask, couple_rate, send_index, live_slots, block_source,
    remap_weight,
):
    shape = jax.ShapeDtypeStruct
    rate = vert_rate.transpose(1, 0, 2)
    packed, mix0, mixr, bulk, tabs, gate = pl.pallas_call(
        mix_kernel,
        out_shape=[
            shape((5, 4, FIELDS, TB), BF16),
            shape((FIELDS, COLS), F32),
            shape((REST, COLS), F32),
            shape((REST, COLS), BF16),
            shape((2 * COLS // TB, 16, TB), BF16),
            shape((FIELDS, COLS), F32),
        ],
        in_specs=[pl.BlockSpec(memory_space=pltpu.HBM)] * 7,
        out_specs=spec(6),
        scratch_shapes=[
            pltpu.VMEM((LEVELS, FIELDS, COLS), F32),
            pltpu.VMEM((LEVELS - 1, 1, COLS), F32),
            pltpu.VMEM((5, 4, TB), jnp.int32),
            pltpu.VMEM((6, 1, COLS), jnp.int32),
            pltpu.VMEM((6, 1, COLS), F32),
            pltpu.VMEM((1, COLS), jnp.int32),
            pltpu.VMEM((1, FIELDS), F32),
            pltpu.SemaphoreType.DMA((8,)),
        ],
        compiler_params=params(PICK_MIB),
        cost_estimate=cost(3),
        name="mix",
    )(
        column_state, rate, send_index[0, 0], hor_offsets.transpose(1, 0, 2), hor_coef.transpose(1, 0, 2), open_mask,
        couple_rate,
    )
    swapped = crossed(packed)

    pair = shape((4, FIELDS, TB), BF16)
    payload = shape((PAY, 16, TB), BF16)
    e1, o1, e2, o2, tabs = pl.pallas_call(
        stage_kernel,
        out_shape=[payload, payload, pair, pair, shape(tabs.shape, BF16)],
        in_specs=spec(2),
        out_specs=spec(5),
        compiler_params=params(4),
        cost_estimate=cost(1),
        name="stage",
    )(swapped, tabs)
    staged = e1
    e1, e2, o1, o2 = paired(e1, 1, False), paired(e2, 2, False), paired(o1, 1, True), paired(o2, 2, True)

    tab = pltpu.VMEM((16, TB), F32)
    rel = pltpu.VMEM((16 * (WIN // LANE), LANE), F32)
    band_own = pl.pallas_call(
        own_band_kernel,
        out_shape=shape((COLS // TB, WIN, TB), BF16),
        in_specs=spec(1) + [ANYWHERE],
        out_specs=spec(1)[0],
        scratch_shapes=[tab, rel],
        compiler_params=params(8),
        cost_estimate=cost(3),
        name="own_band",
    )(tabs, staged)
    bulk_later, band_own, e1, e2, o1, o2 = lax.optimization_barrier((bulk, band_own, e1, e2, o1, o2))
    bulk_e, bulk_o = paired(bulk_later, 1, False), paired(bulk_later, 1, True)

    forcing, top, top_half = pl.pallas_call(
        remap_kernel,
        out_shape=[shape((FIELDS, COLS), F32), shape((FIELDS, COLS), F32), shape((FIELDS, COLS), BF16)],
        in_specs=[SCALARS, SCALARS] + spec(8) + [ANYWHERE],
        out_specs=spec(3),
        scratch_shapes=[pltpu.VMEM((20, FIELDS, TB), BF16)],
        compiler_params=params(8),
        cost_estimate=cost(2),
        name="remap",
    )(
        live_slots[0], block_source[0, 0].T, e1, o1, e2, o2, swapped, remap_weight[0, 0], mix0, gate, band_own,
    )
    top_e, top_o = paired(top_half, 1, False), paired(top_half, 1, True)

    band_side, keep = pl.pallas_call(
        side_band_kernel,
        out_shape=[shape((2 * WIDE // TB, WIN, TB), BF16), shape((1, COLS + 2 * WIDE), F32)],
        in_specs=spec(3) + [ANYWHERE],
        out_specs=spec(2),
        scratch_shapes=[tab, rel],
        compiler_params=params(8),
        cost_estimate=cost(4),
        name="side_band",
    )(e1, tabs, o1, top_half)

    half = pltpu.VMEM((LEVELS * FIELDS, COLS + 2 * WIDE), BF16)
    state = pl.pallas_call(
        diffuse_kernel,
        out_shape=shape((LEVELS * FIELDS, COLS), F32),
        in_specs=spec(11),
        out_specs=pl.BlockSpec(memory_space=pltpu.VMEM),
        scratch_shapes=[half, half, pltpu.VMEM((LEVELS * FIELDS, COLS + 2 * WIDE), F32)],
        compiler_params=params(16),
        cost_estimate=cost(6),
        name="diffuse",
    )(band_own, band_side, keep, mixr, bulk_e, bulk, bulk_o, top, top_e, top_half, top_o)
    return state.reshape(1, LEVELS, FIELDS, COLS), forcing[None]


def solution(mesh):
    placed = (
        P("comp", None, None, "dom"),
        P("comp", None, "dom"),
        P("comp", None, "dom"),
        P("comp", None, "dom"),
        P("comp", "dom"),
        P("comp", None),
        P("comp", "dom", None, None, None),
        P("comp", "dom", None),
        P("comp", "dom", None, None),
        P("comp", "dom", None, None, None, None),
    )
    return jax.shard_map(
        shards,
        mesh=mesh,
        in_specs=placed,
        out_specs=(P("comp", None, None, "dom"), P("comp", None, "dom")),
        check_vma=False,
    )
```

```python
import jax
import jax.numpy as jnp
from jax import lax
from jax.experimental import pallas as pl
from jax.experimental.pallas import tpu as pltpu
from jax.sharding import PartitionSpec as P

F32, BF16 = jnp.float32, jnp.bfloat16
RIM = 512
NSUB = 4
TB = 256
WIN = TB + 2 * RIM
LANE = 128
NEVER = 64.0
FIELDS, LEVELS, COLS = 16, 8, 2048
REST = (LEVELS - 1) * FIELDS
WIDE = COLS - RIM
PICK_MIB = 63
PAY = 4 + 2 * WIDE // TB


def mix_kernel(
    state_hbm, rate_hbm, send_hbm, offs_hbm, coef_hbm, mask_hbm, couple_hbm, packed, mix0, mixr, tabs, gate,
    state, rate, send, offs, coef, mask, couple, sems,
):
    pairs = (
        (state_hbm.at[0, 0:2], state.at[0:2]),
        (rate_hbm, rate),
        (send_hbm, send),
        (offs_hbm, offs),
        (coef_hbm, coef),
        (mask_hbm, mask),
        (couple_hbm, couple),
        (state_hbm.at[0, 2:LEVELS], state.at[2:LEVELS]),
    )
    copies = [pltpu.make_async_copy(a, b, sems.at[i]) for i, (a, b) in enumerate(pairs)]
    for copy in copies:
        copy.start()
    for copy in copies[:3]:
        copy.wait()
    for c in range(0, COLS, TB):
        here = slice(c, c + TB)
        v0 = state[0, :, here]
        mix0[:, here] = v0 + rate[0, :, here] * (state[1, :, here] - v0)
    for k in range(5):
        for j in range(4):
            for h in range(2):
                index = send[k, j : j + 1, h * LANE : (h + 1) * LANE]
                low = jnp.broadcast_to(index & (LANE - 1), (FIELDS, LANE))
                high = jnp.broadcast_to(lax.shift_right_logical(index, 7), (FIELDS, LANE))
                total = jnp.zeros((FIELDS, LANE), F32)
                for p in range(COLS // LANE):
                    got = jnp.take_along_axis(
                        mix0[:, p * LANE : (p + 1) * LANE], low, axis=1, mode="promise_in_bounds"
                    )
                    total = jnp.where(high == p, got, total)
                packed[k, j, :, h * LANE : (h + 1) * LANE] = total.astype(BF16)
    for copy in copies[3:]:
        copy.wait()
    eye = lax.broadcasted_iota(jnp.int32, (FIELDS, FIELDS), 0) == lax.broadcasted_iota(
        jnp.int32, (FIELDS, FIELDS), 1
    )
    couple_column = jnp.sum(
        jnp.where(eye, jnp.broadcast_to(couple[...], (FIELDS, FIELDS)), 0.0), axis=1, keepdims=True
    )
    for n in range(COLS // TB):
        here = slice(n * TB, (n + 1) * TB)
        gate[:, here] = couple_column * mask[0:1, here].astype(F32)
        before = state[0, :, here]
        mid = state[1, :, here]
        flux = rate[0, :, here] * (mid - before)
        for l in range(1, LEVELS):
            if l < LEVELS - 1:
                after_mid = state[l + 1, :, here]
                below = rate[l, :, here] * (after_mid - mid)
                new = mid + below - flux
                flux, mid = below, after_mid
            else:
                new = mid - flux
            mixr[(l - 1) * FIELDS : l * FIELDS, here] = new
        lane = lax.broadcasted_iota(jnp.int32, (1, TB), 1) + RIM
        off = [offs[j, :, here] for j in range(6)]
        val = [coef[j, :, here] for j in range(6)]
        zero = jnp.zeros((1, TB), F32)
        rows_c, rows_h, rows_l = [], [], []
        for j in range(6):
            merged = val[j]
            repeated = zero
            for i in range(6):
                if i != j:
                    same = off[i] == off[j]
                    merged = merged + jnp.where(same, val[i], 0.0)
                    if i < j:
                        repeated = jnp.where(same, 1.0, repeated)
            place = off[j] + lane
            rows_c.append(jnp.where(repeated > 0.5, 0.0, merged))
            rows_h.append(jnp.where(repeated > 0.5, NEVER, lax.shift_right_logical(place, 7).astype(F32)))
            rows_l.append((place & (LANE - 1)).astype(F32))
        tabs[2 * n] = jnp.concatenate(rows_c + [zero] * 2 + rows_h + [zero] * 2, axis=0).astype(BF16)
        tabs[2 * n + 1] = jnp.concatenate(rows_l + [zero] * 10, axis=0).astype(BF16)


def parities():
    d = lax.axis_index("dom")
    return (d & 1) == 0, (d & 2) == 0


def stage_kernel(swapped, tabs, e1, o1, e2, o2, kept):
    near, far = parities()
    e1[0:4] = swapped[jnp.where(near, 3, 1)]
    e1[4:PAY] = tabs[pl.ds(jnp.where(near, 2 * COLS // TB - (PAY - 4), 0), PAY - 4)]
    o1[0:4] = swapped[jnp.where(near, 1, 3)]
    o1[4:PAY] = tabs[pl.ds(jnp.where(near, 0, 2 * COLS // TB - (PAY - 4)), PAY - 4)]
    kept[...] = tabs[...]
    e2[...] = swapped[jnp.where(far, 4, 0)]
    o2[...] = swapped[jnp.where(far, 0, 4)]


def build_bands(tab, rel, band, into, count, tabs, start):
    rows = [
        (lax.broadcasted_iota(jnp.int32, (16, LANE), 0) + r).astype(F32).astype(BF16) for r in range(0, LANE, 16)
    ]

    @pl.loop(0, count)
    def _(b):
        first = tabs[start + 2 * b].astype(F32)
        second = tabs[start + 2 * b + 1].astype(F32)
        tab[0:8] = first[0:8]
        tab[8:16] = first[8:16] * float(LANE) + second[0:8]
        for half in range(TB // LANE):
            lanes = slice(half * LANE, (half + 1) * LANE)
            coefs = [jnp.broadcast_to(tab[j : j + 1, lanes], (16, LANE)).astype(BF16) for j in range(6)]
            first_row = half * LANE
            last_row = first_row + LANE + 2 * RIM
            if first_row:
                band[into + b, 0:first_row, lanes] = jnp.zeros((first_row, LANE), BF16)
            if last_row < WIN:
                band[into + b, last_row:WIN, lanes] = jnp.zeros((WIN - last_row, LANE), BF16)
            for base in range(first_row, last_row, LANE):
                slot = 8 * (half * (WIN // LANE) + base // LANE)
                rel[slot : slot + 8, :] = tab[8:16, lanes] - float(base)
                there = [
                    jnp.broadcast_to(rel[slot + j : slot + j + 1, :], (16, LANE)).astype(BF16) for j in range(6)
                ]
                for r in range(0, LANE, 16):
                    total = jnp.zeros((16, LANE), BF16)
                    for j in range(6):
                        total = jnp.where(there[j] == rows[r // 16], coefs[j], total)
                    band[into + b, base + r : base + r + 16, lanes] = total


def own_band_kernel(tabs, mixr, after, band, bulk, tab, rel):
    del after
    for c in range(0, COLS, TB):
        bulk[:, c : c + TB] = mixr[:, c : c + TB].astype(BF16)
    build_bands(tab, rel, band, 0, COLS // TB, tabs, 0)


def side_band_kernel(e1, tabs, o1, after, band, keep, tab, rel):
    del after
    near, _ = parities()
    side = WIDE // TB
    places = (
        (e1, 4, side, jnp.where(near, WIDE + COLS, 0)),
        (tabs, 0, COLS // TB, WIDE),
        (o1, 4, side, jnp.where(near, 0, WIDE + COLS)),
    )
    for ref, start, count, base in places:
        for b in range(count):
            coefs = ref[start + 2 * b].astype(F32)[0:8]
            at = base + b * TB
            at = at if isinstance(at, int) else pl.multiple_of(at, TB)
            keep[:, pl.ds(at, TB)] = 1.0 - jnp.sum(coefs, axis=0, keepdims=True)
    build_bands(tab, rel, band, 0, side, e1, 4)
    build_bands(tab, rel, band, side, side, o1, 4)


def remap_kernel(live, source, e1, o1, e2, o2, swapped, weights, mix0, gate, after, forcing, top, top_half, got):
    del after
    near, far = parities()
    got[pl.ds(jnp.where(far, 0, 16), 4)] = e2[...]
    got[pl.ds(jnp.where(near, 4, 12), 4)] = e1[0:4]
    got[8:12] = swapped[2]
    got[pl.ds(jnp.where(near, 12, 4), 4)] = o1[0:4]
    got[pl.ds(jnp.where(far, 16, 0), 4)] = o2[...]
    ones = jnp.ones((16, TB), BF16)
    for n in range(COLS // TB):
        here = slice(n * TB, (n + 1) * TB)
        num = jnp.zeros((FIELDS, TB), F32)
        den = jnp.zeros((1, TB), F32)
        for m in range(2):
            q = source[m, n]
            valid = jnp.where((q & 3) < live[0, lax.shift_right_logical(q, 2)], 1.0, 0.0).astype(F32)
            rows = jnp.concatenate([got[q], ones], axis=0)
            both = lax.dot_general(
                rows, weights[n, m], (((1,), (1,)), ((), ())), preferred_element_type=F32
            )
            num = num + valid * both[0:FIELDS]
            den = den + valid * both[FIELDS : FIELDS + 1]
        value = num / jnp.maximum(den, 1.0)
        forcing[:, here] = value
        old = mix0[:, here]
        new = old + gate[:, here] * (value - old)
        top[:, here] = new
        top_half[:, here] = new.astype(BF16)


EDGE = WIDE // TB
OWN = COLS // TB


def part(blocks, source, bands, keep, old, new):
    for b, band in blocks:
        rows = source[:, b * TB : b * TB + WIN]
        at = slice(b * TB, (b + 1) * TB)
        new(b, old(b) * keep[:, at] + jnp.dot(rows, bands(band), preferred_element_type=F32))


def blocks_of(own, side, on_right):
    return [(EDGE + n, ("own", n)) for n in own] + [((EDGE + OWN if on_right else 0) + n, ("side", n)) for n in side]


def per_order(run):
    near, _ = parities()

    @pl.when(near)
    def _():
        run(True)

    @pl.when(jnp.logical_not(near))
    def _():
        run(False)


def begin_kernel(band_own, band_side, keep, mixr, bulk, bulk_e, top, top_half, top_e, st, xa, xb, x0):
    x0[0:FIELDS, COLS : 2 * COLS] = top_half[...]
    x0[FIELDS:, COLS : 2 * COLS] = bulk[...]

    def run(right):
        there = slice(2 * COLS, 3 * COLS) if right else slice(0, COLS)
        x0[0:FIELDS, there] = top_e[...]
        x0[FIELDS:, there] = bulk_e[...]

        def bands(band):
            return band_own[band[1]] if band[0] == "own" else band_side[band[1]]

        for step in range(1, NSUB):
            count = OWN - 2 * step
            own = range(2 * step, OWN) if right else range(0, count)
            side = range(0, count) if right else range(2 * step - 2, EDGE)
            dst = xa if step % 2 else xb

            def old(b):
                if step > 1:
                    return st[:, b * TB : (b + 1) * TB]
                if EDGE <= b < EDGE + OWN:
                    mine = slice((b - EDGE) * TB, (b - EDGE + 1) * TB)
                    return jnp.concatenate([top[:, mine], mixr[:, mine]], axis=0)
                return x0[:, RIM + b * TB : RIM + (b + 1) * TB].astype(F32)

            def new(b, value):
                st[:, b * TB : (b + 1) * TB] = value
                dst[:, RIM + b * TB : RIM + (b + 1) * TB] = value.astype(BF16)

            src = x0 if step == 1 else (xb if step % 2 else xa)
            part(blocks_of(own, side, right), src, bands, keep, old, new)

    per_order(run)


def finish_kernel(
    band_own, band_side, keep, mixr, bulk, bulk_o, top, top_half, top_o, st_in, xa_in, xb_in, out, st, xa, xb, x0,
):
    x0[0:FIELDS, COLS : 2 * COLS] = top_half[...]
    x0[FIELDS:, COLS : 2 * COLS] = bulk[...]

    def run(right):
        there = slice(0, COLS) if right else slice(2 * COLS, 3 * COLS)
        x0[0:FIELDS, there] = top_o[...]
        x0[FIELDS:, there] = bulk_o[...]

        def bands(band):
            return band_own[band[1]] if band[0] == "own" else band_side[EDGE + band[1]]

        for step in range(1, NSUB):
            first = EDGE + (2 * step if right else OWN - 2 * step - 4)
            at = slice(RIM + first * TB, RIM + (first + 4) * TB)
            if step % 2:
                xa[:, at] = xa_in[:, at]
            else:
                xb[:, at] = xb_in[:, at]
        for step in range(1, NSUB + 1):
            own = range(0, 2 * step) if right else range(OWN - 2 * step, OWN)
            side = range(2 * step - 2, EDGE) if right else range(0, OWN - 2 * step)
            before = range(2 * step - 2, 2 * step) if right else range(OWN - 2 * step, OWN - 2 * step + 2)
            dst = xa if step % 2 else xb

            def old(b):
                n = b - EDGE
                if step > 1:
                    return (st_in if n in before else st)[:, b * TB : (b + 1) * TB]
                if 0 <= n < OWN:
                    mine = slice(n * TB, (n + 1) * TB)
                    return jnp.concatenate([top[:, mine], mixr[:, mine]], axis=0)
                return x0[:, RIM + b * TB : RIM + (b + 1) * TB].astype(F32)

            def new(b, value):
                if step == NSUB:
                    out[:, (b - EDGE) * TB : (b - EDGE + 1) * TB] = value
                else:
                    st[:, b * TB : (b + 1) * TB] = value
                    dst[:, RIM + b * TB : RIM + (b + 1) * TB] = value.astype(BF16)

            src = x0 if step == 1 else (xb if step % 2 else xa)
            part(blocks_of(own, side, not right), src, bands, keep, old, new)

    per_order(run)


def crossed(value):
    size = (lax.axis_size("comp"), lax.axis_size("dom"))
    pairs = [(s * size[1] + d, (1 - s) * size[1] + d) for s in range(size[0]) for d in range(size[1])]
    return lax.ppermute(value, ("comp", "dom"), pairs)


def paired(value, apart, odd):
    count = lax.axis_size("dom")
    pairs = [(d, (d + (apart if bool(d & apart) == odd else -apart)) % count) for d in range(count)]
    return lax.ppermute(value, "dom", pairs)


def spec(n):
    return [pl.BlockSpec(memory_space=pltpu.VMEM)] * n


ANYWHERE = pl.BlockSpec(memory_space=pl.ANY)
SCALARS = pl.BlockSpec(memory_space=pltpu.SMEM)


def params(mib):
    return pltpu.CompilerParams(vmem_limit_bytes=mib * 2**20)


def cost(us):
    return pl.CostEstimate(flops=us * 1_000_000_000, bytes_accessed=us * 3_000_000, transcendentals=0)


def shards(
    column_state, vert_rate, hor_offsets, hor_coef, open_mask, couple_rate, send_index, live_slots, block_source,
    remap_weight,
):
    shape = jax.ShapeDtypeStruct
    rate = vert_rate.transpose(1, 0, 2)
    packed, mix0, mixr, tabs, gate = pl.pallas_call(
        mix_kernel,
        out_shape=[
            shape((5, 4, FIELDS, TB), BF16),
            shape((FIELDS, COLS), F32),
            shape((REST, COLS), F32),
            shape((2 * COLS // TB, 16, TB), BF16),
            shape((FIELDS, COLS), F32),
        ],
        in_specs=[pl.BlockSpec(memory_space=pltpu.HBM)] * 7,
        out_specs=spec(5),
        scratch_shapes=[
            pltpu.VMEM((LEVELS, FIELDS, COLS), F32),
            pltpu.VMEM((LEVELS - 1, 1, COLS), F32),
            pltpu.VMEM((5, 4, TB), jnp.int32),
            pltpu.VMEM((6, 1, COLS), jnp.int32),
            pltpu.VMEM((6, 1, COLS), F32),
            pltpu.VMEM((1, COLS), jnp.int32),
            pltpu.VMEM((1, FIELDS), F32),
            pltpu.SemaphoreType.DMA((8,)),
        ],
        compiler_params=params(PICK_MIB),
        cost_estimate=cost(3),
        name="mix",
    )(
        column_state, rate, send_index[0, 0], hor_offsets.transpose(1, 0, 2), hor_coef.transpose(1, 0, 2), open_mask,
        couple_rate,
    )
    swapped = crossed(packed)

    pair = shape((4, FIELDS, TB), BF16)
    payload = shape((PAY, 16, TB), BF16)
    e1, o1, e2, o2, tabs = pl.pallas_call(
        stage_kernel,
        out_shape=[payload, payload, pair, pair, shape(tabs.shape, BF16)],
        in_specs=spec(2),
        out_specs=spec(5),
        compiler_params=params(4),
        cost_estimate=cost(1),
        name="stage",
    )(swapped, tabs)
    staged = e1
    e1, e2, o1, o2 = paired(e1, 1, False), paired(e2, 2, False), paired(o1, 1, True), paired(o2, 2, True)

    tab = pltpu.VMEM((16, TB), F32)
    rel = pltpu.VMEM((16 * (WIN // LANE), LANE), F32)
    band_own, bulk = pl.pallas_call(
        own_band_kernel,
        out_shape=[shape((COLS // TB, WIN, TB), BF16), shape((REST, COLS), BF16)],
        in_specs=spec(2) + [ANYWHERE],
        out_specs=spec(2),
        scratch_shapes=[tab, rel],
        compiler_params=params(8),
        cost_estimate=cost(3),
        name="own_band",
    )(tabs, mixr, staged)
    bulk_later, e1, e2 = lax.optimization_barrier((bulk, e1, e2))
    bulk_e, bulk_o = paired(bulk_later, 1, False), paired(bulk_later, 1, True)

    forcing, top, top_half = pl.pallas_call(
        remap_kernel,
        out_shape=[shape((FIELDS, COLS), F32), shape((FIELDS, COLS), F32), shape((FIELDS, COLS), BF16)],
        in_specs=[SCALARS, SCALARS] + spec(8) + [ANYWHERE],
        out_specs=spec(3),
        scratch_shapes=[pltpu.VMEM((20, FIELDS, TB), BF16)],
        compiler_params=params(8),
        cost_estimate=cost(20),
        name="remap",
    )(
        live_slots[0], block_source[0, 0].T, e1, o1, e2, o2, swapped, remap_weight[0, 0], mix0, gate, band_own,
    )
    top_e, top_o = paired(top_half, 1, False), paired(top_half, 1, True)

    band_side, keep = pl.pallas_call(
        side_band_kernel,
        out_shape=[shape((2 * WIDE // TB, WIN, TB), BF16), shape((1, COLS + 2 * WIDE), F32)],
        in_specs=spec(3) + [ANYWHERE],
        out_specs=spec(2),
        scratch_shapes=[tab, rel],
        compiler_params=params(8),
        cost_estimate=cost(1),
        name="side_band",
    )(e1, tabs, o1, top_half)

    wide = (LEVELS * FIELDS, 3 * COLS)
    narrow = (LEVELS * FIELDS, COLS + 2 * WIDE)
    st, xa, xb = pl.pallas_call(
        begin_kernel,
        out_shape=[shape(narrow, F32), shape(wide, BF16), shape(wide, BF16)],
        in_specs=spec(9),
        out_specs=spec(3),
        scratch_shapes=[pltpu.VMEM(wide, BF16)],
        compiler_params=params(8),
        cost_estimate=cost(1),
        name="begin",
    )(band_own, band_side, keep, mixr, bulk, bulk_e, top, top_half, top_e)
    state = pl.pallas_call(
        finish_kernel,
        out_shape=shape((LEVELS * FIELDS, COLS), F32),
        in_specs=spec(12),
        out_specs=pl.BlockSpec(memory_space=pltpu.VMEM),
        scratch_shapes=[
            pltpu.VMEM(narrow, F32), pltpu.VMEM(wide, BF16), pltpu.VMEM(wide, BF16), pltpu.VMEM(wide, BF16),
        ],
        compiler_params=params(16),
        cost_estimate=cost(4),
        name="finish",
    )(band_own, band_side, keep, mixr, bulk, bulk_o, top, top_half, top_o, st, xa, xb)
    return state.reshape(1, LEVELS, FIELDS, COLS), forcing[None]


def solution(mesh):
    placed = (
        P("comp", None, None, "dom"),
        P("comp", None, "dom"),
        P("comp", None, "dom"),
        P("comp", None, "dom"),
        P("comp", "dom"),
        P("comp", None),
        P("comp", "dom", None, None, None),
        P("comp", "dom", None),
        P("comp", "dom", None, None),
        P("comp", "dom", None, None, None, None),
    )
    return jax.shard_map(
        shards,
        mesh=mesh,
        in_specs=placed,
        out_specs=(P("comp", None, None, "dom"), P("comp", None, "dom")),
        check_vma=False,
    )
```

```python
import jax
import jax.numpy as jnp
from jax import lax
from jax.experimental import pallas as pl
from jax.experimental.pallas import tpu as pltpu
from jax.sharding import PartitionSpec as P

F32, BF16 = jnp.float32, jnp.bfloat16
RIM = 512
NSUB = 4
TB = 256
WIN = TB + 2 * RIM
LANE = 128
NEVER = 64.0
FIELDS, LEVELS, COLS = 16, 8, 2048
REST = (LEVELS - 1) * FIELDS
WIDE = COLS - RIM
PICK_MIB = 63
PAY = 4 + 2 * WIDE // TB


def mix_kernel(
    state_hbm, rate_hbm, send_hbm, offs_hbm, coef_hbm, mask_hbm, couple_hbm, packed, mix0, mixr, tabs, gate,
    state, rate, send, offs, coef, mask, couple, sems,
):
    pairs = (
        (state_hbm.at[0, 0:2], state.at[0:2]),
        (rate_hbm, rate),
        (send_hbm, send),
        (offs_hbm, offs),
        (coef_hbm, coef),
        (mask_hbm, mask),
        (couple_hbm, couple),
        (state_hbm.at[0, 2:LEVELS], state.at[2:LEVELS]),
    )
    copies = [pltpu.make_async_copy(a, b, sems.at[i]) for i, (a, b) in enumerate(pairs)]
    for copy in copies:
        copy.start()
    for copy in copies[:3]:
        copy.wait()
    for c in range(0, COLS, TB):
        here = slice(c, c + TB)
        v0 = state[0, :, here]
        mix0[:, here] = v0 + rate[0, :, here] * (state[1, :, here] - v0)
    for k in range(5):
        for j in range(4):
            for h in range(2):
                index = send[k, j : j + 1, h * LANE : (h + 1) * LANE]
                low = jnp.broadcast_to(index & (LANE - 1), (FIELDS, LANE))
                high = jnp.broadcast_to(lax.shift_right_logical(index, 7), (FIELDS, LANE))
                total = jnp.zeros((FIELDS, LANE), F32)
                for p in range(COLS // LANE):
                    got = jnp.take_along_axis(
                        mix0[:, p * LANE : (p + 1) * LANE], low, axis=1, mode="promise_in_bounds"
                    )
                    total = jnp.where(high == p, got, total)
                packed[k, j, :, h * LANE : (h + 1) * LANE] = total.astype(BF16)
    for copy in copies[3:]:
        copy.wait()
    eye = lax.broadcasted_iota(jnp.int32, (FIELDS, FIELDS), 0) == lax.broadcasted_iota(
        jnp.int32, (FIELDS, FIELDS), 1
    )
    couple_column = jnp.sum(
        jnp.where(eye, jnp.broadcast_to(couple[...], (FIELDS, FIELDS)), 0.0), axis=1, keepdims=True
    )
    for n in range(COLS // TB):
        here = slice(n * TB, (n + 1) * TB)
        gate[:, here] = couple_column * mask[0:1, here].astype(F32)
        before = state[0, :, here]
        mid = state[1, :, here]
        flux = rate[0, :, here] * (mid - before)
        for l in range(1, LEVELS):
            if l < LEVELS - 1:
                after_mid = state[l + 1, :, here]
                below = rate[l, :, here] * (after_mid - mid)
                new = mid + below - flux
                flux, mid = below, after_mid
            else:
                new = mid - flux
            mixr[(l - 1) * FIELDS : l * FIELDS, here] = new
        lane = lax.broadcasted_iota(jnp.int32, (1, TB), 1) + RIM
        off = [offs[j, :, here] for j in range(6)]
        val = [coef[j, :, here] for j in range(6)]
        zero = jnp.zeros((1, TB), F32)
        rows_c, rows_h, rows_l = [], [], []
        for j in range(6):
            merged = val[j]
            repeated = zero
            for i in range(6):
                if i != j:
                    same = off[i] == off[j]
                    merged = merged + jnp.where(same, val[i], 0.0)
                    if i < j:
                        repeated = jnp.where(same, 1.0, repeated)
            place = off[j] + lane
            rows_c.append(jnp.where(repeated > 0.5, 0.0, merged))
            rows_h.append(jnp.where(repeated > 0.5, NEVER, lax.shift_right_logical(place, 7).astype(F32)))
            rows_l.append((place & (LANE - 1)).astype(F32))
        tabs[2 * n] = jnp.concatenate(rows_c + [zero] * 2 + rows_h + [zero] * 2, axis=0).astype(BF16)
        tabs[2 * n + 1] = jnp.concatenate(rows_l + [zero] * 10, axis=0).astype(BF16)


def parities():
    d = lax.axis_index("dom")
    return (d & 1) == 0, (d & 2) == 0


def hold_kernel(tabs, kept):
    kept[...] = tabs[...]


def stage_kernel(swapped, tabs, e1, o1, e2, o2):
    near, far = parities()
    e1[0:4] = swapped[jnp.where(near, 3, 1)]
    e1[4:PAY] = tabs[pl.ds(jnp.where(near, 2 * COLS // TB - (PAY - 4), 0), PAY - 4)]
    o1[0:4] = swapped[jnp.where(near, 1, 3)]
    o1[4:PAY] = tabs[pl.ds(jnp.where(near, 0, 2 * COLS // TB - (PAY - 4)), PAY - 4)]
    e2[...] = swapped[jnp.where(far, 4, 0)]
    o2[...] = swapped[jnp.where(far, 0, 4)]


def build_bands(tab, rel, band, into, count, tabs, start):
    rows = [
        (lax.broadcasted_iota(jnp.int32, (16, LANE), 0) + r).astype(F32).astype(BF16) for r in range(0, LANE, 16)
    ]

    @pl.loop(0, count)
    def _(b):
        first = tabs[start + 2 * b].astype(F32)
        second = tabs[start + 2 * b + 1].astype(F32)
        tab[0:8] = first[0:8]
        tab[8:16] = first[8:16] * float(LANE) + second[0:8]
        for half in range(TB // LANE):
            lanes = slice(half * LANE, (half + 1) * LANE)
            coefs = [jnp.broadcast_to(tab[j : j + 1, lanes], (16, LANE)).astype(BF16) for j in range(6)]
            first_row = half * LANE
            last_row = first_row + LANE + 2 * RIM
            if first_row:
                band[into + b, 0:first_row, lanes] = jnp.zeros((first_row, LANE), BF16)
            if last_row < WIN:
                band[into + b, last_row:WIN, lanes] = jnp.zeros((WIN - last_row, LANE), BF16)
            for base in range(first_row, last_row, LANE):
                slot = 8 * (half * (WIN // LANE) + base // LANE)
                rel[slot : slot + 8, :] = tab[8:16, lanes] - float(base)
                there = [
                    jnp.broadcast_to(rel[slot + j : slot + j + 1, :], (16, LANE)).astype(BF16) for j in range(6)
                ]
                for r in range(0, LANE, 16):
                    total = jnp.zeros((16, LANE), BF16)
                    for j in range(6):
                        total = jnp.where(there[j] == rows[r // 16], coefs[j], total)
                    band[into + b, base + r : base + r + 16, lanes] = total


def own_band_kernel(tabs, mixr, after, band, bulk, tab, rel):
    del after
    for c in range(0, COLS, TB):
        bulk[:, c : c + TB] = mixr[:, c : c + TB].astype(BF16)
    build_bands(tab, rel, band, 0, COLS // TB, tabs, 0)


def side_band_kernel(e1, tabs, o1, after, band, keep, tab, rel):
    del after
    near, _ = parities()
    side = WIDE // TB
    places = (
        (e1, 4, side, jnp.where(near, WIDE + COLS, 0)),
        (tabs, 0, COLS // TB, WIDE),
        (o1, 4, side, jnp.where(near, 0, WIDE + COLS)),
    )
    for ref, start, count, base in places:
        for b in range(count):
            coefs = ref[start + 2 * b].astype(F32)[0:8]
            at = base + b * TB
            at = at if isinstance(at, int) else pl.multiple_of(at, TB)
            keep[:, pl.ds(at, TB)] = 1.0 - jnp.sum(coefs, axis=0, keepdims=True)
    build_bands(tab, rel, band, 0, side, e1, 4)
    build_bands(tab, rel, band, side, side, o1, 4)


def remap_kernel(live, source, e1, o1, e2, o2, swapped, weights, mix0, gate, after, forcing, top, top_half, got):
    del after
    near, far = parities()
    got[pl.ds(jnp.where(far, 0, 16), 4)] = e2[...]
    got[pl.ds(jnp.where(near, 4, 12), 4)] = e1[0:4]
    got[8:12] = swapped[2]
    got[pl.ds(jnp.where(near, 12, 4), 4)] = o1[0:4]
    got[pl.ds(jnp.where(far, 16, 0), 4)] = o2[...]
    ones = jnp.ones((16, TB), BF16)
    for n in range(COLS // TB):
        here = slice(n * TB, (n + 1) * TB)
        num = jnp.zeros((FIELDS, TB), F32)
        den = jnp.zeros((1, TB), F32)
        for m in range(2):
            q = source[m, n]
            valid = jnp.where((q & 3) < live[0, lax.shift_right_logical(q, 2)], 1.0, 0.0).astype(F32)
            rows = jnp.concatenate([got[q], ones], axis=0)
            both = lax.dot_general(
                rows, weights[n, m], (((1,), (1,)), ((), ())), preferred_element_type=F32
            )
            num = num + valid * both[0:FIELDS]
            den = den + valid * both[FIELDS : FIELDS + 1]
        value = num / jnp.maximum(den, 1.0)
        forcing[:, here] = value
        old = mix0[:, here]
        new = old + gate[:, here] * (value - old)
        top[:, here] = new
        top_half[:, here] = new.astype(BF16)


EDGE = WIDE // TB
OWN = COLS // TB


def part(blocks, source, bands, keep, old, new):
    for b, band in blocks:
        rows = source[:, b * TB : b * TB + WIN]
        at = slice(b * TB, (b + 1) * TB)
        new(b, old(b) * keep[:, at] + jnp.dot(rows, bands(band), preferred_element_type=F32))


def blocks_of(own, side, on_right):
    return [(EDGE + n, ("own", n)) for n in own] + [((EDGE + OWN if on_right else 0) + n, ("side", n)) for n in side]


def per_order(run):
    near, _ = parities()

    @pl.when(near)
    def _():
        run(True)

    @pl.when(jnp.logical_not(near))
    def _():
        run(False)


def begin_kernel(band_own, band_side, keep, mixr, bulk, bulk_e, top, top_half, top_e, st, xa, xb, x0):
    x0[0:FIELDS, COLS : 2 * COLS] = top_half[...]
    x0[FIELDS:, COLS : 2 * COLS] = bulk[...]

    def run(right):
        there = slice(2 * COLS, 3 * COLS) if right else slice(0, COLS)
        x0[0:FIELDS, there] = top_e[...]
        x0[FIELDS:, there] = bulk_e[...]

        def bands(band):
            return band_own[band[1]] if band[0] == "own" else band_side[band[1]]

        for step in range(1, NSUB):
            count = OWN - 2 * step
            own = range(2 * step, OWN) if right else range(0, count)
            side = range(0, count) if right else range(2 * step - 2, EDGE)
            dst = xa if step % 2 else xb

            def old(b):
                if step > 1:
                    return st[:, b * TB : (b + 1) * TB]
                if EDGE <= b < EDGE + OWN:
                    mine = slice((b - EDGE) * TB, (b - EDGE + 1) * TB)
                    return jnp.concatenate([top[:, mine], mixr[:, mine]], axis=0)
                return x0[:, RIM + b * TB : RIM + (b + 1) * TB].astype(F32)

            def new(b, value):
                st[:, b * TB : (b + 1) * TB] = value
                dst[:, RIM + b * TB : RIM + (b + 1) * TB] = value.astype(BF16)

            src = x0 if step == 1 else (xb if step % 2 else xa)
            part(blocks_of(own, side, right), src, bands, keep, old, new)

    per_order(run)


def finish_kernel(
    band_own, band_side, keep, mixr, bulk, bulk_o, top, top_half, top_o, st_in, xa_in, xb_in, out, st, xa, xb, x0, result,
    sems,
):
    x0[0:FIELDS, COLS : 2 * COLS] = top_half[...]
    x0[FIELDS:, COLS : 2 * COLS] = bulk[...]

    def run(right):
        there = slice(0, COLS) if right else slice(2 * COLS, 3 * COLS)
        x0[0:FIELDS, there] = top_o[...]
        x0[FIELDS:, there] = bulk_o[...]

        def bands(band):
            return band_own[band[1]] if band[0] == "own" else band_side[EDGE + band[1]]

        for step in range(1, NSUB):
            first = EDGE + (2 * step if right else OWN - 2 * step - 4)
            at = slice(RIM + first * TB, RIM + (first + 4) * TB)
            if step % 2:
                xa[:, at] = xa_in[:, at]
            else:
                xb[:, at] = xb_in[:, at]
        for step in range(1, NSUB + 1):
            own = range(0, 2 * step) if right else range(OWN - 2 * step, OWN)
            side = range(2 * step - 2, EDGE) if right else range(0, OWN - 2 * step)
            before = range(2 * step - 2, 2 * step) if right else range(OWN - 2 * step, OWN - 2 * step + 2)
            dst = xa if step % 2 else xb

            def old(b):
                n = b - EDGE
                if step > 1:
                    return (st_in if n in before else st)[:, b * TB : (b + 1) * TB]
                if 0 <= n < OWN:
                    mine = slice(n * TB, (n + 1) * TB)
                    return jnp.concatenate([top[:, mine], mixr[:, mine]], axis=0)
                return x0[:, RIM + b * TB : RIM + (b + 1) * TB].astype(F32)

            def new(b, value):
                if step == NSUB:
                    mine = slice((b - EDGE) * TB, (b - EDGE + 1) * TB)
                    result[:, mine] = value
                    pltpu.make_async_copy(result.at[:, mine], out.at[:, mine], sems.at[b - EDGE]).start()
                else:
                    st[:, b * TB : (b + 1) * TB] = value
                    dst[:, RIM + b * TB : RIM + (b + 1) * TB] = value.astype(BF16)

            src = x0 if step == 1 else (xb if step % 2 else xa)
            part(blocks_of(own, side, not right), src, bands, keep, old, new)

    per_order(run)
    for n in range(OWN):
        mine = slice(n * TB, (n + 1) * TB)
        pltpu.make_async_copy(result.at[:, mine], out.at[:, mine], sems.at[n]).wait()


def crossed(value):
    size = (lax.axis_size("comp"), lax.axis_size("dom"))
    pairs = [(s * size[1] + d, (1 - s) * size[1] + d) for s in range(size[0]) for d in range(size[1])]
    return lax.ppermute(value, ("comp", "dom"), pairs)


def paired(value, apart, odd):
    count = lax.axis_size("dom")
    pairs = [(d, (d + (apart if bool(d & apart) == odd else -apart)) % count) for d in range(count)]
    return lax.ppermute(value, "dom", pairs)


def spec(n):
    return [pl.BlockSpec(memory_space=pltpu.VMEM)] * n


ANYWHERE = pl.BlockSpec(memory_space=pl.ANY)
SCALARS = pl.BlockSpec(memory_space=pltpu.SMEM)


def params(mib):
    return pltpu.CompilerParams(vmem_limit_bytes=mib * 2**20)


def cost(us):
    return pl.CostEstimate(flops=us * 1_000_000_000, bytes_accessed=us * 3_000_000, transcendentals=0)


def shards(
    column_state, vert_rate, hor_offsets, hor_coef, open_mask, couple_rate, send_index, live_slots, block_source,
    remap_weight,
):
    shape = jax.ShapeDtypeStruct
    rate = vert_rate.transpose(1, 0, 2)
    packed, mix0, mixr, tabs, gate = pl.pallas_call(
        mix_kernel,
        out_shape=[
            shape((5, 4, FIELDS, TB), BF16),
            shape((FIELDS, COLS), F32),
            shape((REST, COLS), F32),
            shape((2 * COLS // TB, 16, TB), BF16),
            shape((FIELDS, COLS), F32),
        ],
        in_specs=[pl.BlockSpec(memory_space=pltpu.HBM)] * 7,
        out_specs=spec(5),
        scratch_shapes=[
            pltpu.VMEM((LEVELS, FIELDS, COLS), F32),
            pltpu.VMEM((LEVELS - 1, 1, COLS), F32),
            pltpu.VMEM((5, 4, TB), jnp.int32),
            pltpu.VMEM((6, 1, COLS), jnp.int32),
            pltpu.VMEM((6, 1, COLS), F32),
            pltpu.VMEM((1, COLS), jnp.int32),
            pltpu.VMEM((1, FIELDS), F32),
            pltpu.SemaphoreType.DMA((8,)),
        ],
        compiler_params=params(PICK_MIB),
        cost_estimate=cost(3),
        name="mix",
    )(
        column_state, rate, send_index[0, 0], hor_offsets.transpose(1, 0, 2), hor_coef.transpose(1, 0, 2), open_mask,
        couple_rate,
    )
    swapped = crossed(packed)

    tabs = pl.pallas_call(
        hold_kernel,
        out_shape=shape(tabs.shape, BF16),
        in_specs=spec(1),
        out_specs=spec(1)[0],
        compiler_params=params(4),
        cost_estimate=cost(1),
        name="hold",
    )(tabs)
    pair = shape((4, FIELDS, TB), BF16)
    payload = shape((PAY, 16, TB), BF16)
    e1, o1, e2, o2 = pl.pallas_call(
        stage_kernel,
        out_shape=[payload, payload, pair, pair],
        in_specs=spec(2),
        out_specs=spec(4),
        compiler_params=params(4),
        cost_estimate=cost(1),
        name="stage",
    )(swapped, tabs)
    staged = e1
    e1, e2, o1, o2 = paired(e1, 1, False), paired(e2, 2, False), paired(o1, 1, True), paired(o2, 2, True)

    tab = pltpu.VMEM((16, TB), F32)
    rel = pltpu.VMEM((16 * (WIN // LANE), LANE), F32)
    band_own, bulk = pl.pallas_call(
        own_band_kernel,
        out_shape=[shape((COLS // TB, WIN, TB), BF16), shape((REST, COLS), BF16)],
        in_specs=spec(2) + [ANYWHERE],
        out_specs=spec(2),
        scratch_shapes=[tab, rel],
        compiler_params=params(8),
        cost_estimate=cost(3),
        name="own_band",
    )(tabs, mixr, staged)
    bulk_later, e2 = lax.optimization_barrier((bulk, e2))
    bulk_e, bulk_o = paired(bulk_later, 1, False), paired(bulk_later, 1, True)

    forcing, top, top_half = pl.pallas_call(
        remap_kernel,
        out_shape=[shape((FIELDS, COLS), F32), shape((FIELDS, COLS), F32), shape((FIELDS, COLS), BF16)],
        in_specs=[SCALARS, SCALARS] + spec(8) + [ANYWHERE],
        out_specs=spec(3),
        scratch_shapes=[pltpu.VMEM((20, FIELDS, TB), BF16)],
        compiler_params=params(8),
        cost_estimate=cost(20),
        name="remap",
    )(
        live_slots[0], block_source[0, 0].T, e1, o1, e2, o2, swapped, remap_weight[0, 0], mix0, gate, band_own,
    )
    top_e, top_o = paired(top_half, 1, False), paired(top_half, 1, True)

    band_side, keep = pl.pallas_call(
        side_band_kernel,
        out_shape=[shape((2 * WIDE // TB, WIN, TB), BF16), shape((1, COLS + 2 * WIDE), F32)],
        in_specs=spec(3) + [ANYWHERE],
        out_specs=spec(2),
        scratch_shapes=[tab, rel],
        compiler_params=params(8),
        cost_estimate=cost(1),
        name="side_band",
    )(e1, tabs, o1, top_half)

    wide = (LEVELS * FIELDS, 3 * COLS)
    narrow = (LEVELS * FIELDS, COLS + 2 * WIDE)
    st, xa, xb = pl.pallas_call(
        begin_kernel,
        out_shape=[shape(narrow, F32), shape(wide, BF16), shape(wide, BF16)],
        in_specs=spec(9),
        out_specs=spec(3),
        scratch_shapes=[pltpu.VMEM(wide, BF16)],
        compiler_params=params(8),
        cost_estimate=cost(1),
        name="begin",
    )(band_own, band_side, keep, mixr, bulk, bulk_e, top, top_half, top_e)
    state = pl.pallas_call(
        finish_kernel,
        out_shape=shape((LEVELS * FIELDS, COLS), F32),
        in_specs=spec(12),
        out_specs=ANYWHERE,
        scratch_shapes=[
            pltpu.VMEM(narrow, F32), pltpu.VMEM(wide, BF16), pltpu.VMEM(wide, BF16), pltpu.VMEM(wide, BF16),
            pltpu.VMEM((LEVELS * FIELDS, COLS), F32), pltpu.SemaphoreType.DMA((OWN,)),
        ],
        compiler_params=params(16),
        cost_estimate=cost(4),
        name="finish",
    )(band_own, band_side, keep, mixr, bulk, bulk_o, top, top_half, top_o, st, xa, xb)
    return state.reshape(1, LEVELS, FIELDS, COLS), forcing[None]


def solution(mesh):
    placed = (
        P("comp", None, None, "dom"),
        P("comp", None, "dom"),
        P("comp", None, "dom"),
        P("comp", None, "dom"),
        P("comp", "dom"),
        P("comp", None),
        P("comp", "dom", None, None, None),
        P("comp", "dom", None),
        P("comp", "dom", None, None),
        P("comp", "dom", None, None, None, None),
    )
    return jax.shard_map(
        shards,
        mesh=mesh,
        in_specs=placed,
        out_specs=(P("comp", None, None, "dom"), P("comp", None, "dom")),
        check_vma=False,
    )
```

```python
import jax
import jax.numpy as jnp
from jax import lax
from jax.experimental import pallas as pl
from jax.experimental.pallas import tpu as pltpu
from jax.sharding import PartitionSpec as P

F32, BF16 = jnp.float32, jnp.bfloat16
RIM = 512
NSUB = 4
TB = 256
WIN = TB + 2 * RIM
LANE = 128
NEVER = 64.0
FIELDS, LEVELS, COLS = 16, 8, 2048
REST = (LEVELS - 1) * FIELDS
WIDE = COLS - RIM
PICK_MIB = 63
PAY = 4 + 2 * WIDE // TB


def mix_kernel(
    state_hbm, rate_hbm, send_hbm, offs_hbm, coef_hbm, mask_hbm, couple_hbm, packed, mix0, mixr, sent, tabs, gate,
    state, rate, send, offs, coef, mask, couple, sems,
):
    pairs = (
        (state_hbm.at[0, 0:2], state.at[0:2]),
        (rate_hbm, rate),
        (send_hbm, send),
        (offs_hbm, offs),
        (coef_hbm, coef),
        (mask_hbm, mask),
        (couple_hbm, couple),
        (state_hbm.at[0, 2:LEVELS], state.at[2:LEVELS]),
    )
    copies = [pltpu.make_async_copy(a, b, sems.at[i]) for i, (a, b) in enumerate(pairs)]
    for copy in copies:
        copy.start()
    for copy in copies[:3]:
        copy.wait()
    for c in range(0, COLS, TB):
        here = slice(c, c + TB)
        v0 = state[0, :, here]
        mix0[:, here] = v0 + rate[0, :, here] * (state[1, :, here] - v0)
    for k in range(5):
        for j in range(4):
            for h in range(2):
                index = send[k, j : j + 1, h * LANE : (h + 1) * LANE]
                low = jnp.broadcast_to(index & (LANE - 1), (FIELDS, LANE))
                high = jnp.broadcast_to(lax.shift_right_logical(index, 7), (FIELDS, LANE))
                total = jnp.zeros((FIELDS, LANE), F32)
                for p in range(COLS // LANE):
                    got = jnp.take_along_axis(
                        mix0[:, p * LANE : (p + 1) * LANE], low, axis=1, mode="promise_in_bounds"
                    )
                    total = jnp.where(high == p, got, total)
                packed[k, j, :, h * LANE : (h + 1) * LANE] = total.astype(BF16)
    for copy in copies[3:]:
        copy.wait()
    eye = lax.broadcasted_iota(jnp.int32, (FIELDS, FIELDS), 0) == lax.broadcasted_iota(
        jnp.int32, (FIELDS, FIELDS), 1
    )
    couple_column = jnp.sum(
        jnp.where(eye, jnp.broadcast_to(couple[...], (FIELDS, FIELDS)), 0.0), axis=1, keepdims=True
    )
    for n in range(COLS // TB):
        here = slice(n * TB, (n + 1) * TB)
        gate[:, here] = couple_column * mask[0:1, here].astype(F32)
        before = state[0, :, here]
        mid = state[1, :, here]
        flux = rate[0, :, here] * (mid - before)
        for l in range(1, LEVELS):
            if l < LEVELS - 1:
                after_mid = state[l + 1, :, here]
                below = rate[l, :, here] * (after_mid - mid)
                new = mid + below - flux
                flux, mid = below, after_mid
            else:
                new = mid - flux
            mixr[(l - 1) * FIELDS : l * FIELDS, here] = new
            sent[(l - 1) * FIELDS : l * FIELDS, here] = new.astype(BF16)
        lane = lax.broadcasted_iota(jnp.int32, (1, TB), 1) + RIM
        off = [offs[j, :, here] for j in range(6)]
        val = [coef[j, :, here] for j in range(6)]
        zero = jnp.zeros((1, TB), F32)
        rows_c, rows_h, rows_l = [], [], []
        for j in range(6):
            merged = val[j]
            repeated = zero
            for i in range(6):
                if i != j:
                    same = off[i] == off[j]
                    merged = merged + jnp.where(same, val[i], 0.0)
                    if i < j:
                        repeated = jnp.where(same, 1.0, repeated)
            place = off[j] + lane
            rows_c.append(jnp.where(repeated > 0.5, 0.0, merged))
            rows_h.append(jnp.where(repeated > 0.5, NEVER, lax.shift_right_logical(place, 7).astype(F32)))
            rows_l.append((place & (LANE - 1)).astype(F32))
        tabs[2 * n] = jnp.concatenate(rows_c + [zero] * 2 + rows_h + [zero] * 2, axis=0).astype(BF16)
        tabs[2 * n + 1] = jnp.concatenate(rows_l + [zero] * 10, axis=0).astype(BF16)


def parities():
    d = lax.axis_index("dom")
    return (d & 1) == 0, (d & 2) == 0


def hold_kernel(tabs, kept):
    kept[...] = tabs[...]


def stage_kernel(swapped, tabs, e1, o1, e2, o2):
    near, far = parities()
    e1[0:4] = swapped[jnp.where(near, 3, 1)]
    e1[4:PAY] = tabs[pl.ds(jnp.where(near, 2 * COLS // TB - (PAY - 4), 0), PAY - 4)]
    o1[0:4] = swapped[jnp.where(near, 1, 3)]
    o1[4:PAY] = tabs[pl.ds(jnp.where(near, 0, 2 * COLS // TB - (PAY - 4)), PAY - 4)]
    e2[...] = swapped[jnp.where(far, 4, 0)]
    o2[...] = swapped[jnp.where(far, 0, 4)]


def build_bands(tab, rel, band, into, count, tabs, start):
    rows = [
        (lax.broadcasted_iota(jnp.int32, (16, LANE), 0) + r).astype(F32).astype(BF16) for r in range(0, LANE, 16)
    ]

    @pl.loop(0, count)
    def _(b):
        first = tabs[start + 2 * b].astype(F32)
        second = tabs[start + 2 * b + 1].astype(F32)
        tab[0:8] = first[0:8]
        tab[8:16] = first[8:16] * float(LANE) + second[0:8]
        for half in range(TB // LANE):
            lanes = slice(half * LANE, (half + 1) * LANE)
            coefs = [jnp.broadcast_to(tab[j : j + 1, lanes], (16, LANE)).astype(BF16) for j in range(6)]
            first_row = half * LANE
            last_row = first_row + LANE + 2 * RIM
            if first_row:
                band[into + b, 0:first_row, lanes] = jnp.zeros((first_row, LANE), BF16)
            if last_row < WIN:
                band[into + b, last_row:WIN, lanes] = jnp.zeros((WIN - last_row, LANE), BF16)
            for base in range(first_row, last_row, LANE):
                slot = 8 * (half * (WIN // LANE) + base // LANE)
                rel[slot : slot + 8, :] = tab[8:16, lanes] - float(base)
                there = [
                    jnp.broadcast_to(rel[slot + j : slot + j + 1, :], (16, LANE)).astype(BF16) for j in range(6)
                ]
                for r in range(0, LANE, 16):
                    total = jnp.zeros((16, LANE), BF16)
                    for j in range(6):
                        total = jnp.where(there[j] == rows[r // 16], coefs[j], total)
                    band[into + b, base + r : base + r + 16, lanes] = total


def own_band_kernel(tabs, mixr, after, band, bulk, tab, rel):
    del after
    for c in range(0, COLS, TB):
        bulk[:, c : c + TB] = mixr[:, c : c + TB].astype(BF16)
    build_bands(tab, rel, band, 0, COLS // TB, tabs, 0)


def side_band_kernel(e1, tabs, o1, after, band, keep, tab, rel):
    del after
    near, _ = parities()
    side = WIDE // TB
    places = (
        (e1, 4, side, jnp.where(near, WIDE + COLS, 0)),
        (tabs, 0, COLS // TB, WIDE),
        (o1, 4, side, jnp.where(near, 0, WIDE + COLS)),
    )
    for ref, start, count, base in places:
        for b in range(count):
            coefs = ref[start + 2 * b].astype(F32)[0:8]
            at = base + b * TB
            at = at if isinstance(at, int) else pl.multiple_of(at, TB)
            keep[:, pl.ds(at, TB)] = 1.0 - jnp.sum(coefs, axis=0, keepdims=True)
    build_bands(tab, rel, band, 0, side, e1, 4)
    build_bands(tab, rel, band, side, side, o1, 4)


def remap_kernel(live, source, e1, o1, e2, o2, swapped, weights, mix0, gate, after, forcing, top, top_half, got):
    del after
    near, far = parities()
    got[pl.ds(jnp.where(far, 0, 16), 4)] = e2[...]
    got[pl.ds(jnp.where(near, 4, 12), 4)] = e1[0:4]
    got[8:12] = swapped[2]
    got[pl.ds(jnp.where(near, 12, 4), 4)] = o1[0:4]
    got[pl.ds(jnp.where(far, 16, 0), 4)] = o2[...]
    ones = jnp.ones((16, TB), BF16)
    for n in range(COLS // TB):
        here = slice(n * TB, (n + 1) * TB)
        num = jnp.zeros((FIELDS, TB), F32)
        den = jnp.zeros((1, TB), F32)
        for m in range(2):
            q = source[m, n]
            valid = jnp.where((q & 3) < live[0, lax.shift_right_logical(q, 2)], 1.0, 0.0).astype(F32)
            rows = jnp.concatenate([got[q], ones], axis=0)
            both = lax.dot_general(
                rows, weights[n, m], (((1,), (1,)), ((), ())), preferred_element_type=F32
            )
            num = num + valid * both[0:FIELDS]
            den = den + valid * both[FIELDS : FIELDS + 1]
        value = num / jnp.maximum(den, 1.0)
        forcing[:, here] = value
        old = mix0[:, here]
        new = old + gate[:, here] * (value - old)
        top[:, here] = new
        top_half[:, here] = new.astype(BF16)


EDGE = WIDE // TB
OWN = COLS // TB


def part(blocks, source, bands, keep, old, new):
    for b, band in blocks:
        rows = source[:, b * TB : b * TB + WIN]
        at = slice(b * TB, (b + 1) * TB)
        new(b, old(b) * keep[:, at] + jnp.dot(rows, bands(band), preferred_element_type=F32))


def blocks_of(own, side, on_right):
    return [(EDGE + n, ("own", n)) for n in own] + [((EDGE + OWN if on_right else 0) + n, ("side", n)) for n in side]


def per_order(run):
    near, _ = parities()

    @pl.when(near)
    def _():
        run(True)

    @pl.when(jnp.logical_not(near))
    def _():
        run(False)


def begin_kernel(band_own, band_side, keep, mixr, bulk, bulk_e, top, top_half, top_e, st, xa, xb, x0):
    x0[0:FIELDS, COLS : 2 * COLS] = top_half[...]
    x0[FIELDS:, COLS : 2 * COLS] = bulk[...]

    def run(right):
        there = slice(2 * COLS, 3 * COLS) if right else slice(0, COLS)
        x0[0:FIELDS, there] = top_e[...]
        x0[FIELDS:, there] = bulk_e[...]

        def bands(band):
            return band_own[band[1]] if band[0] == "own" else band_side[band[1]]

        for step in range(1, NSUB):
            count = OWN - 2 * step
            own = range(2 * step, OWN) if right else range(0, count)
            side = range(0, count) if right else range(2 * step - 2, EDGE)
            dst = xa if step % 2 else xb

            def old(b):
                if step > 1:
                    return st[:, b * TB : (b + 1) * TB]
                if EDGE <= b < EDGE + OWN:
                    mine = slice((b - EDGE) * TB, (b - EDGE + 1) * TB)
                    return jnp.concatenate([top[:, mine], mixr[:, mine]], axis=0)
                return x0[:, RIM + b * TB : RIM + (b + 1) * TB].astype(F32)

            def new(b, value):
                st[:, b * TB : (b + 1) * TB] = value
                dst[:, RIM + b * TB : RIM + (b + 1) * TB] = value.astype(BF16)

            src = x0 if step == 1 else (xb if step % 2 else xa)
            part(blocks_of(own, side, right), src, bands, keep, old, new)

    per_order(run)


def finish_kernel(
    band_own, band_side, keep, mixr, bulk, bulk_o, top, top_half, top_o, st_in, xa_in, xb_in, out, st, xa, xb, x0, result,
    sems,
):
    x0[0:FIELDS, COLS : 2 * COLS] = top_half[...]
    x0[FIELDS:, COLS : 2 * COLS] = bulk[...]

    def run(right):
        there = slice(0, COLS) if right else slice(2 * COLS, 3 * COLS)
        x0[0:FIELDS, there] = top_o[...]
        x0[FIELDS:, there] = bulk_o[...]

        def bands(band):
            return band_own[band[1]] if band[0] == "own" else band_side[EDGE + band[1]]

        for step in range(1, NSUB):
            first = EDGE + (2 * step if right else OWN - 2 * step - 4)
            at = slice(RIM + first * TB, RIM + (first + 4) * TB)
            if step % 2:
                xa[:, at] = xa_in[:, at]
            else:
                xb[:, at] = xb_in[:, at]
        for step in range(1, NSUB + 1):
            own = range(0, 2 * step) if right else range(OWN - 2 * step, OWN)
            side = range(2 * step - 2, EDGE) if right else range(0, OWN - 2 * step)
            before = range(2 * step - 2, 2 * step) if right else range(OWN - 2 * step, OWN - 2 * step + 2)
            dst = xa if step % 2 else xb

            def old(b):
                n = b - EDGE
                if step > 1:
                    return (st_in if n in before else st)[:, b * TB : (b + 1) * TB]
                if 0 <= n < OWN:
                    mine = slice(n * TB, (n + 1) * TB)
                    return jnp.concatenate([top[:, mine], mixr[:, mine]], axis=0)
                return x0[:, RIM + b * TB : RIM + (b + 1) * TB].astype(F32)

            def new(b, value):
                if step == NSUB:
                    mine = slice((b - EDGE) * TB, (b - EDGE + 1) * TB)
                    result[:, mine] = value
                    pltpu.make_async_copy(result.at[:, mine], out.at[:, mine], sems.at[b - EDGE]).start()
                else:
                    st[:, b * TB : (b + 1) * TB] = value
                    dst[:, RIM + b * TB : RIM + (b + 1) * TB] = value.astype(BF16)

            src = x0 if step == 1 else (xb if step % 2 else xa)
            part(blocks_of(own, side, not right), src, bands, keep, old, new)

    per_order(run)
    for n in range(OWN):
        mine = slice(n * TB, (n + 1) * TB)
        pltpu.make_async_copy(result.at[:, mine], out.at[:, mine], sems.at[n]).wait()


def crossed(value):
    size = (lax.axis_size("comp"), lax.axis_size("dom"))
    pairs = [(s * size[1] + d, (1 - s) * size[1] + d) for s in range(size[0]) for d in range(size[1])]
    return lax.ppermute(value, ("comp", "dom"), pairs)


def paired(value, apart, odd):
    count = lax.axis_size("dom")
    pairs = [(d, (d + (apart if bool(d & apart) == odd else -apart)) % count) for d in range(count)]
    return lax.ppermute(value, "dom", pairs)


def spec(n):
    return [pl.BlockSpec(memory_space=pltpu.VMEM)] * n


ANYWHERE = pl.BlockSpec(memory_space=pl.ANY)
SCALARS = pl.BlockSpec(memory_space=pltpu.SMEM)


def params(mib):
    return pltpu.CompilerParams(vmem_limit_bytes=mib * 2**20)


def cost(us):
    return pl.CostEstimate(flops=us * 1_000_000_000, bytes_accessed=us * 3_000_000, transcendentals=0)


def shards(
    column_state, vert_rate, hor_offsets, hor_coef, open_mask, couple_rate, send_index, live_slots, block_source,
    remap_weight,
):
    shape = jax.ShapeDtypeStruct
    rate = vert_rate.transpose(1, 0, 2)
    packed, mix0, mixr, sent, tabs, gate = pl.pallas_call(
        mix_kernel,
        out_shape=[
            shape((5, 4, FIELDS, TB), BF16),
            shape((FIELDS, COLS), F32),
            shape((REST, COLS), F32),
            shape((REST, COLS), BF16),
            shape((2 * COLS // TB, 16, TB), BF16),
            shape((FIELDS, COLS), F32),
        ],
        in_specs=[pl.BlockSpec(memory_space=pltpu.HBM)] * 7,
        out_specs=spec(6),
        scratch_shapes=[
            pltpu.VMEM((LEVELS, FIELDS, COLS), F32),
            pltpu.VMEM((LEVELS - 1, 1, COLS), F32),
            pltpu.VMEM((5, 4, TB), jnp.int32),
            pltpu.VMEM((6, 1, COLS), jnp.int32),
            pltpu.VMEM((6, 1, COLS), F32),
            pltpu.VMEM((1, COLS), jnp.int32),
            pltpu.VMEM((1, FIELDS), F32),
            pltpu.SemaphoreType.DMA((8,)),
        ],
        compiler_params=params(PICK_MIB),
        cost_estimate=cost(3),
        name="mix",
    )(
        column_state, rate, send_index[0, 0], hor_offsets.transpose(1, 0, 2), hor_coef.transpose(1, 0, 2), open_mask,
        couple_rate,
    )
    swapped = crossed(packed)

    tabs = pl.pallas_call(
        hold_kernel,
        out_shape=shape(tabs.shape, BF16),
        in_specs=spec(1),
        out_specs=spec(1)[0],
        compiler_params=params(4),
        cost_estimate=cost(1),
        name="hold",
    )(tabs)
    pair = shape((4, FIELDS, TB), BF16)
    payload = shape((PAY, 16, TB), BF16)
    e1, o1, e2, o2 = pl.pallas_call(
        stage_kernel,
        out_shape=[payload, payload, pair, pair],
        in_specs=spec(2),
        out_specs=spec(4),
        compiler_params=params(4),
        cost_estimate=cost(1),
        name="stage",
    )(swapped, tabs)
    staged = e1
    e1, e2, o1, o2 = paired(e1, 1, False), paired(e2, 2, False), paired(o1, 1, True), paired(o2, 2, True)

    bulk_later, e2 = lax.optimization_barrier((sent, e2))
    bulk_e, bulk_o = paired(bulk_later, 1, False), paired(bulk_later, 1, True)

    tab = pltpu.VMEM((16, TB), F32)
    rel = pltpu.VMEM((16 * (WIN // LANE), LANE), F32)
    band_own, bulk = pl.pallas_call(
        own_band_kernel,
        out_shape=[shape((COLS // TB, WIN, TB), BF16), shape((REST, COLS), BF16)],
        in_specs=spec(2) + [ANYWHERE],
        out_specs=spec(2),
        scratch_shapes=[tab, rel],
        compiler_params=params(8),
        cost_estimate=cost(3),
        name="own_band",
    )(tabs, mixr, e1)

    forcing, top, top_half = pl.pallas_call(
        remap_kernel,
        out_shape=[shape((FIELDS, COLS), F32), shape((FIELDS, COLS), F32), shape((FIELDS, COLS), BF16)],
        in_specs=[SCALARS, SCALARS] + spec(8) + [ANYWHERE],
        out_specs=spec(3),
        scratch_shapes=[pltpu.VMEM((20, FIELDS, TB), BF16)],
        compiler_params=params(8),
        cost_estimate=cost(20),
        name="remap",
    )(
        live_slots[0], block_source[0, 0].T, e1, o1, e2, o2, swapped, remap_weight[0, 0], mix0, gate, band_own,
    )
    top_e, top_o = paired(top_half, 1, False), paired(top_half, 1, True)

    band_side, keep = pl.pallas_call(
        side_band_kernel,
        out_shape=[shape((2 * WIDE // TB, WIN, TB), BF16), shape((1, COLS + 2 * WIDE), F32)],
        in_specs=spec(3) + [ANYWHERE],
        out_specs=spec(2),
        scratch_shapes=[tab, rel],
        compiler_params=params(8),
        cost_estimate=cost(1),
        name="side_band",
    )(e1, tabs, o1, top_half)

    wide = (LEVELS * FIELDS, 3 * COLS)
    narrow = (LEVELS * FIELDS, COLS + 2 * WIDE)
    st, xa, xb = pl.pallas_call(
        begin_kernel,
        out_shape=[shape(narrow, F32), shape(wide, BF16), shape(wide, BF16)],
        in_specs=spec(9),
        out_specs=spec(3),
        scratch_shapes=[pltpu.VMEM(wide, BF16)],
        compiler_params=params(8),
        cost_estimate=cost(1),
        name="begin",
    )(band_own, band_side, keep, mixr, bulk, bulk_e, top, top_half, top_e)
    state = pl.pallas_call(
        finish_kernel,
        out_shape=shape((LEVELS * FIELDS, COLS), F32),
        in_specs=spec(12),
        out_specs=ANYWHERE,
        scratch_shapes=[
            pltpu.VMEM(narrow, F32), pltpu.VMEM(wide, BF16), pltpu.VMEM(wide, BF16), pltpu.VMEM(wide, BF16),
            pltpu.VMEM((LEVELS * FIELDS, COLS), F32), pltpu.SemaphoreType.DMA((OWN,)),
        ],
        compiler_params=params(16),
        cost_estimate=cost(4),
        name="finish",
    )(band_own, band_side, keep, mixr, bulk, bulk_o, top, top_half, top_o, st, xa, xb)
    return state.reshape(1, LEVELS, FIELDS, COLS), forcing[None]


def solution(mesh):
    placed = (
        P("comp", None, None, "dom"),
        P("comp", None, "dom"),
        P("comp", None, "dom"),
        P("comp", None, "dom"),
        P("comp", "dom"),
        P("comp", None),
        P("comp", "dom", None, None, None),
        P("comp", "dom", None),
        P("comp", "dom", None, None),
        P("comp", "dom", None, None, None, None),
    )
    return jax.shard_map(
        shards,
        mesh=mesh,
        in_specs=placed,
        out_specs=(P("comp", None, None, "dom"), P("comp", None, "dom")),
        check_vma=False,
    )
```

```python
import jax
import jax.numpy as jnp
from jax import lax
from jax.experimental import pallas as pl
from jax.experimental.pallas import tpu as pltpu
from jax.sharding import PartitionSpec as P

F32, BF16 = jnp.float32, jnp.bfloat16
RIM = 512
NSUB = 4
TB = 256
WIN = TB + 2 * RIM
LANE = 128
NEVER = 64.0
FIELDS, LEVELS, COLS = 16, 8, 2048
REST = (LEVELS - 1) * FIELDS
WIDE = COLS - RIM
PICK_MIB = 63
EARLY = 4
PAY = 4 + 2 * WIDE // TB


def mix_kernel(
    state_hbm, rate_hbm, send_hbm, offs_hbm, coef_hbm, mask_hbm, couple_hbm, packed, mix0, mixr, tabs, gate,
    state, rate, send, offs, coef, mask, couple, sems,
):
    pairs = (
        (state_hbm.at[0, 0:2], state.at[0:2]),
        (rate_hbm, rate),
        (send_hbm, send),
        (offs_hbm, offs),
        (coef_hbm, coef),
        (mask_hbm, mask),
        (couple_hbm, couple),
        (state_hbm.at[0, 2:LEVELS], state.at[2:LEVELS]),
    )
    copies = [pltpu.make_async_copy(a, b, sems.at[i]) for i, (a, b) in enumerate(pairs)]
    for copy in copies:
        copy.start()
    for copy in copies[:3]:
        copy.wait()
    for c in range(0, COLS, TB):
        here = slice(c, c + TB)
        v0 = state[0, :, here]
        mix0[:, here] = v0 + rate[0, :, here] * (state[1, :, here] - v0)
    for k in range(5):
        for j in range(4):
            for h in range(2):
                index = send[k, j : j + 1, h * LANE : (h + 1) * LANE]
                low = jnp.broadcast_to(index & (LANE - 1), (FIELDS, LANE))
                high = jnp.broadcast_to(lax.shift_right_logical(index, 7), (FIELDS, LANE))
                total = jnp.zeros((FIELDS, LANE), F32)
                for p in range(COLS // LANE):
                    got = jnp.take_along_axis(
                        mix0[:, p * LANE : (p + 1) * LANE], low, axis=1, mode="promise_in_bounds"
                    )
                    total = jnp.where(high == p, got, total)
                packed[k, j, :, h * LANE : (h + 1) * LANE] = total.astype(BF16)
    for copy in copies[3:]:
        copy.wait()
    eye = lax.broadcasted_iota(jnp.int32, (FIELDS, FIELDS), 0) == lax.broadcasted_iota(
        jnp.int32, (FIELDS, FIELDS), 1
    )
    couple_column = jnp.sum(
        jnp.where(eye, jnp.broadcast_to(couple[...], (FIELDS, FIELDS)), 0.0), axis=1, keepdims=True
    )
    for n in range(COLS // TB):
        here = slice(n * TB, (n + 1) * TB)
        gate[:, here] = couple_column * mask[0:1, here].astype(F32)
        before = state[0, :, here]
        mid = state[1, :, here]
        flux = rate[0, :, here] * (mid - before)
        for l in range(1, LEVELS):
            if l < LEVELS - 1:
                after_mid = state[l + 1, :, here]
                below = rate[l, :, here] * (after_mid - mid)
                new = mid + below - flux
                flux, mid = below, after_mid
            else:
                new = mid - flux
            mixr[(l - 1) * FIELDS : l * FIELDS, here] = new
        lane = lax.broadcasted_iota(jnp.int32, (1, TB), 1) + RIM
        off = [offs[j, :, here] for j in range(6)]
        val = [coef[j, :, here] for j in range(6)]
        zero = jnp.zeros((1, TB), F32)
        rows_c, rows_h, rows_l = [], [], []
        for j in range(6):
            merged = val[j]
            repeated = zero
            for i in range(6):
                if i != j:
                    same = off[i] == off[j]
                    merged = merged + jnp.where(same, val[i], 0.0)
                    if i < j:
                        repeated = jnp.where(same, 1.0, repeated)
            place = off[j] + lane
            rows_c.append(jnp.where(repeated > 0.5, 0.0, merged))
            rows_h.append(jnp.where(repeated > 0.5, NEVER, lax.shift_right_logical(place, 7).astype(F32)))
            rows_l.append((place & (LANE - 1)).astype(F32))
        tabs[2 * n] = jnp.concatenate(rows_c + [zero] * 2 + rows_h + [zero] * 2, axis=0).astype(BF16)
        tabs[2 * n + 1] = jnp.concatenate(rows_l + [zero] * 10, axis=0).astype(BF16)


def parities():
    d = lax.axis_index("dom")
    return (d & 1) == 0, (d & 2) == 0


def hold_kernel(tabs, kept):
    kept[...] = tabs[...]


def stage_kernel(swapped, tabs, e1, o1, e2, o2):
    near, far = parities()
    e1[0:4] = swapped[jnp.where(near, 3, 1)]
    e1[4:PAY] = tabs[pl.ds(jnp.where(near, 2 * COLS // TB - (PAY - 4), 0), PAY - 4)]
    o1[0:4] = swapped[jnp.where(near, 1, 3)]
    o1[4:PAY] = tabs[pl.ds(jnp.where(near, 0, 2 * COLS // TB - (PAY - 4)), PAY - 4)]
    e2[...] = swapped[jnp.where(far, 4, 0)]
    o2[...] = swapped[jnp.where(far, 0, 4)]


def build_bands(tab, rel, band, into, count, tabs, start):
    rows = [
        (lax.broadcasted_iota(jnp.int32, (16, LANE), 0) + r).astype(F32).astype(BF16) for r in range(0, LANE, 16)
    ]

    @pl.loop(0, count)
    def _(b):
        first = tabs[start + 2 * b].astype(F32)
        second = tabs[start + 2 * b + 1].astype(F32)
        tab[0:8] = first[0:8]
        tab[8:16] = first[8:16] * float(LANE) + second[0:8]
        for half in range(TB // LANE):
            lanes = slice(half * LANE, (half + 1) * LANE)
            coefs = [jnp.broadcast_to(tab[j : j + 1, lanes], (16, LANE)).astype(BF16) for j in range(6)]
            first_row = half * LANE
            last_row = first_row + LANE + 2 * RIM
            if first_row:
                band[into + b, 0:first_row, lanes] = jnp.zeros((first_row, LANE), BF16)
            if last_row < WIN:
                band[into + b, last_row:WIN, lanes] = jnp.zeros((WIN - last_row, LANE), BF16)
            for base in range(first_row, last_row, LANE):
                slot = 8 * (half * (WIN // LANE) + base // LANE)
                rel[slot : slot + 8, :] = tab[8:16, lanes] - float(base)
                there = [
                    jnp.broadcast_to(rel[slot + j : slot + j + 1, :], (16, LANE)).astype(BF16) for j in range(6)
                ]
                for r in range(0, LANE, 16):
                    total = jnp.zeros((16, LANE), BF16)
                    for j in range(6):
                        total = jnp.where(there[j] == rows[r // 16], coefs[j], total)
                    band[into + b, base + r : base + r + 16, lanes] = total


def own_band_kernel(tabs, mixr, after, band, bulk, tab, rel):
    del after
    for c in range(0, COLS, TB):
        bulk[:, c : c + TB] = mixr[:, c : c + TB].astype(BF16)
    build_bands(tab, rel, band, 0, EARLY, tabs, 0)


def side_band_kernel(e1, tabs, o1, after, band, late, keep, tab, rel):
    del after
    near, _ = parities()
    side = WIDE // TB
    places = (
        (e1, 4, side, jnp.where(near, WIDE + COLS, 0)),
        (tabs, 0, COLS // TB, WIDE),
        (o1, 4, side, jnp.where(near, 0, WIDE + COLS)),
    )
    for ref, start, count, base in places:
        for b in range(count):
            coefs = ref[start + 2 * b].astype(F32)[0:8]
            at = base + b * TB
            at = at if isinstance(at, int) else pl.multiple_of(at, TB)
            keep[:, pl.ds(at, TB)] = 1.0 - jnp.sum(coefs, axis=0, keepdims=True)
    build_bands(tab, rel, band, 0, side, e1, 4)
    build_bands(tab, rel, band, side, side, o1, 4)
    build_bands(tab, rel, late, 0, COLS // TB - EARLY, tabs, 2 * EARLY)


def remap_kernel(live, source, e1, o1, e2, o2, swapped, weights, mix0, gate, after, forcing, top, top_half, got):
    del after
    near, far = parities()
    got[pl.ds(jnp.where(far, 0, 16), 4)] = e2[...]
    got[pl.ds(jnp.where(near, 4, 12), 4)] = e1[0:4]
    got[8:12] = swapped[2]
    got[pl.ds(jnp.where(near, 12, 4), 4)] = o1[0:4]
    got[pl.ds(jnp.where(far, 16, 0), 4)] = o2[...]
    ones = jnp.ones((16, TB), BF16)
    for n in range(COLS // TB):
        here = slice(n * TB, (n + 1) * TB)
        num = jnp.zeros((FIELDS, TB), F32)
        den = jnp.zeros((1, TB), F32)
        for m in range(2):
            q = source[m, n]
            valid = jnp.where((q & 3) < live[0, lax.shift_right_logical(q, 2)], 1.0, 0.0).astype(F32)
            rows = jnp.concatenate([got[q], ones], axis=0)
            both = lax.dot_general(
                rows, weights[n, m], (((1,), (1,)), ((), ())), preferred_element_type=F32
            )
            num = num + valid * both[0:FIELDS]
            den = den + valid * both[FIELDS : FIELDS + 1]
        value = num / jnp.maximum(den, 1.0)
        forcing[:, here] = value
        old = mix0[:, here]
        new = old + gate[:, here] * (value - old)
        top[:, here] = new
        top_half[:, here] = new.astype(BF16)


EDGE = WIDE // TB
OWN = COLS // TB


def part(blocks, source, bands, keep, old, new):
    for b, band in blocks:
        rows = source[:, b * TB : b * TB + WIN]
        at = slice(b * TB, (b + 1) * TB)
        new(b, old(b) * keep[:, at] + jnp.dot(rows, bands(band), preferred_element_type=F32))


def blocks_of(own, side, on_right):
    return [(EDGE + n, ("own", n)) for n in own] + [((EDGE + OWN if on_right else 0) + n, ("side", n)) for n in side]


def own_band(early, late, n):
    return early[n] if n < EARLY else late[n - EARLY]


def per_order(run):
    near, _ = parities()

    @pl.when(near)
    def _():
        run(True)

    @pl.when(jnp.logical_not(near))
    def _():
        run(False)


def begin_kernel(band_own, band_late, band_side, keep, mixr, bulk, bulk_e, top, top_half, top_e, st, xa, xb, x0):
    x0[0:FIELDS, COLS : 2 * COLS] = top_half[...]
    x0[FIELDS:, COLS : 2 * COLS] = bulk[...]

    def run(right):
        there = slice(2 * COLS, 3 * COLS) if right else slice(0, COLS)
        x0[0:FIELDS, there] = top_e[...]
        x0[FIELDS:, there] = bulk_e[...]

        def bands(band):
            return own_band(band_own, band_late, band[1]) if band[0] == "own" else band_side[band[1]]

        for step in range(1, NSUB):
            count = OWN - 2 * step
            own = range(2 * step, OWN) if right else range(0, count)
            side = range(0, count) if right else range(2 * step - 2, EDGE)
            dst = xa if step % 2 else xb

            def old(b):
                if step > 1:
                    return st[:, b * TB : (b + 1) * TB]
                if EDGE <= b < EDGE + OWN:
                    mine = slice((b - EDGE) * TB, (b - EDGE + 1) * TB)
                    return jnp.concatenate([top[:, mine], mixr[:, mine]], axis=0)
                return x0[:, RIM + b * TB : RIM + (b + 1) * TB].astype(F32)

            def new(b, value):
                st[:, b * TB : (b + 1) * TB] = value
                dst[:, RIM + b * TB : RIM + (b + 1) * TB] = value.astype(BF16)

            src = x0 if step == 1 else (xb if step % 2 else xa)
            part(blocks_of(own, side, right), src, bands, keep, old, new)

    per_order(run)


def finish_kernel(
    band_own, band_late, band_side, keep, mixr, bulk, bulk_o, top, top_half, top_o, st_in, xa_in, xb_in, out, st, xa, xb, x0, result,
    sems,
):
    x0[0:FIELDS, COLS : 2 * COLS] = top_half[...]
    x0[FIELDS:, COLS : 2 * COLS] = bulk[...]

    def run(right):
        there = slice(0, COLS) if right else slice(2 * COLS, 3 * COLS)
        x0[0:FIELDS, there] = top_o[...]
        x0[FIELDS:, there] = bulk_o[...]

        def bands(band):
            return own_band(band_own, band_late, band[1]) if band[0] == "own" else band_side[EDGE + band[1]]

        for step in range(1, NSUB):
            first = EDGE + (2 * step if right else OWN - 2 * step - 4)
            at = slice(RIM + first * TB, RIM + (first + 4) * TB)
            if step % 2:
                xa[:, at] = xa_in[:, at]
            else:
                xb[:, at] = xb_in[:, at]
        for step in range(1, NSUB + 1):
            own = range(0, 2 * step) if right else range(OWN - 2 * step, OWN)
            side = range(2 * step - 2, EDGE) if right else range(0, OWN - 2 * step)
            before = range(2 * step - 2, 2 * step) if right else range(OWN - 2 * step, OWN - 2 * step + 2)
            dst = xa if step % 2 else xb

            def old(b):
                n = b - EDGE
                if step > 1:
                    return (st_in if n in before else st)[:, b * TB : (b + 1) * TB]
                if 0 <= n < OWN:
                    mine = slice(n * TB, (n + 1) * TB)
                    return jnp.concatenate([top[:, mine], mixr[:, mine]], axis=0)
                return x0[:, RIM + b * TB : RIM + (b + 1) * TB].astype(F32)

            def new(b, value):
                if step == NSUB:
                    mine = slice((b - EDGE) * TB, (b - EDGE + 1) * TB)
                    result[:, mine] = value
                    pltpu.make_async_copy(result.at[:, mine], out.at[:, mine], sems.at[b - EDGE]).start()
                else:
                    st[:, b * TB : (b + 1) * TB] = value
                    dst[:, RIM + b * TB : RIM + (b + 1) * TB] = value.astype(BF16)

            src = x0 if step == 1 else (xb if step % 2 else xa)
            part(blocks_of(own, side, not right), src, bands, keep, old, new)

    per_order(run)
    for n in range(OWN):
        mine = slice(n * TB, (n + 1) * TB)
        pltpu.make_async_copy(result.at[:, mine], out.at[:, mine], sems.at[n]).wait()


def crossed(value):
    size = (lax.axis_size("comp"), lax.axis_size("dom"))
    pairs = [(s * size[1] + d, (1 - s) * size[1] + d) for s in range(size[0]) for d in range(size[1])]
    return lax.ppermute(value, ("comp", "dom"), pairs)


def paired(value, apart, odd):
    count = lax.axis_size("dom")
    pairs = [(d, (d + (apart if bool(d & apart) == odd else -apart)) % count) for d in range(count)]
    return lax.ppermute(value, "dom", pairs)


def spec(n):
    return [pl.BlockSpec(memory_space=pltpu.VMEM)] * n


ANYWHERE = pl.BlockSpec(memory_space=pl.ANY)
SCALARS = pl.BlockSpec(memory_space=pltpu.SMEM)


def params(mib):
    return pltpu.CompilerParams(vmem_limit_bytes=mib * 2**20)


def cost(us):
    return pl.CostEstimate(flops=us * 1_000_000_000, bytes_accessed=us * 3_000_000, transcendentals=0)


def shards(
    column_state, vert_rate, hor_offsets, hor_coef, open_mask, couple_rate, send_index, live_slots, block_source,
    remap_weight,
):
    shape = jax.ShapeDtypeStruct
    rate = vert_rate.transpose(1, 0, 2)
    packed, mix0, mixr, tabs, gate = pl.pallas_call(
        mix_kernel,
        out_shape=[
            shape((5, 4, FIELDS, TB), BF16),
            shape((FIELDS, COLS), F32),
            shape((REST, COLS), F32),
            shape((2 * COLS // TB, 16, TB), BF16),
            shape((FIELDS, COLS), F32),
        ],
        in_specs=[pl.BlockSpec(memory_space=pltpu.HBM)] * 7,
        out_specs=spec(5),
        scratch_shapes=[
            pltpu.VMEM((LEVELS, FIELDS, COLS), F32),
            pltpu.VMEM((LEVELS - 1, 1, COLS), F32),
            pltpu.VMEM((5, 4, TB), jnp.int32),
            pltpu.VMEM((6, 1, COLS), jnp.int32),
            pltpu.VMEM((6, 1, COLS), F32),
            pltpu.VMEM((1, COLS), jnp.int32),
            pltpu.VMEM((1, FIELDS), F32),
            pltpu.SemaphoreType.DMA((8,)),
        ],
        compiler_params=params(PICK_MIB),
        cost_estimate=cost(3),
        name="mix",
    )(
        column_state, rate, send_index[0, 0], hor_offsets.transpose(1, 0, 2), hor_coef.transpose(1, 0, 2), open_mask,
        couple_rate,
    )
    swapped = crossed(packed)

    tabs = pl.pallas_call(
        hold_kernel,
        out_shape=shape(tabs.shape, BF16),
        in_specs=spec(1),
        out_specs=spec(1)[0],
        compiler_params=params(4),
        cost_estimate=cost(1),
        name="hold",
    )(tabs)
    pair = shape((4, FIELDS, TB), BF16)
    payload = shape((PAY, 16, TB), BF16)
    e1, o1, e2, o2 = pl.pallas_call(
        stage_kernel,
        out_shape=[payload, payload, pair, pair],
        in_specs=spec(2),
        out_specs=spec(4),
        compiler_params=params(4),
        cost_estimate=cost(1),
        name="stage",
    )(swapped, tabs)
    staged = e1
    e1, e2, o1, o2 = paired(e1, 1, False), paired(e2, 2, False), paired(o1, 1, True), paired(o2, 2, True)

    tab = pltpu.VMEM((16, TB), F32)
    rel = pltpu.VMEM((16 * (WIN // LANE), LANE), F32)
    band_own, bulk = pl.pallas_call(
        own_band_kernel,
        out_shape=[shape((EARLY, WIN, TB), BF16), shape((REST, COLS), BF16)],
        in_specs=spec(2) + [ANYWHERE],
        out_specs=spec(2),
        scratch_shapes=[tab, rel],
        compiler_params=params(8),
        cost_estimate=cost(3),
        name="own_band",
    )(tabs, mixr, staged)
    bulk_later, e2 = lax.optimization_barrier((bulk, e2))
    bulk_e, bulk_o = paired(bulk_later, 1, False), paired(bulk_later, 1, True)

    forcing, top, top_half = pl.pallas_call(
        remap_kernel,
        out_shape=[shape((FIELDS, COLS), F32), shape((FIELDS, COLS), F32), shape((FIELDS, COLS), BF16)],
        in_specs=[SCALARS, SCALARS] + spec(8) + [ANYWHERE],
        out_specs=spec(3),
        scratch_shapes=[pltpu.VMEM((20, FIELDS, TB), BF16)],
        compiler_params=params(8),
        cost_estimate=cost(20),
        name="remap",
    )(
        live_slots[0], block_source[0, 0].T, e1, o1, e2, o2, swapped, remap_weight[0, 0], mix0, gate, band_own,
    )
    top_e, top_o = paired(top_half, 1, False), paired(top_half, 1, True)

    band_side, band_late, keep = pl.pallas_call(
        side_band_kernel,
        out_shape=[shape((2 * WIDE // TB, WIN, TB), BF16), shape((OWN - EARLY, WIN, TB), BF16), shape((1, COLS + 2 * WIDE), F32)],
        in_specs=spec(3) + [ANYWHERE],
        out_specs=spec(3),
        scratch_shapes=[tab, rel],
        compiler_params=params(8),
        cost_estimate=cost(1),
        name="side_band",
    )(e1, tabs, o1, top_half)

    wide = (LEVELS * FIELDS, 3 * COLS)
    narrow = (LEVELS * FIELDS, COLS + 2 * WIDE)
    st, xa, xb = pl.pallas_call(
        begin_kernel,
        out_shape=[shape(narrow, F32), shape(wide, BF16), shape(wide, BF16)],
        in_specs=spec(10),
        out_specs=spec(3),
        scratch_shapes=[pltpu.VMEM(wide, BF16)],
        compiler_params=params(8),
        cost_estimate=cost(1),
        name="begin",
    )(band_own, band_late, band_side, keep, mixr, bulk, bulk_e, top, top_half, top_e)
    state = pl.pallas_call(
        finish_kernel,
        out_shape=shape((LEVELS * FIELDS, COLS), F32),
        in_specs=spec(13),
        out_specs=ANYWHERE,
        scratch_shapes=[
            pltpu.VMEM(narrow, F32), pltpu.VMEM(wide, BF16), pltpu.VMEM(wide, BF16), pltpu.VMEM(wide, BF16),
            pltpu.VMEM((LEVELS * FIELDS, COLS), F32), pltpu.SemaphoreType.DMA((OWN,)),
        ],
        compiler_params=params(16),
        cost_estimate=cost(4),
        name="finish",
    )(band_own, band_late, band_side, keep, mixr, bulk, bulk_o, top, top_half, top_o, st, xa, xb)
    return state.reshape(1, LEVELS, FIELDS, COLS), forcing[None]


def solution(mesh):
    placed = (
        P("comp", None, None, "dom"),
        P("comp", None, "dom"),
        P("comp", None, "dom"),
        P("comp", None, "dom"),
        P("comp", "dom"),
        P("comp", None),
        P("comp", "dom", None, None, None),
        P("comp", "dom", None),
        P("comp", "dom", None, None),
        P("comp", "dom", None, None, None, None),
    )
    return jax.shard_map(
        shards,
        mesh=mesh,
        in_specs=placed,
        out_specs=(P("comp", None, None, "dom"), P("comp", None, "dom")),
        check_vma=False,
    )
```

```python
import jax
import jax.numpy as jnp
from jax import lax
from jax.experimental import pallas as pl
from jax.experimental.pallas import tpu as pltpu
from jax.sharding import PartitionSpec as P

F32, BF16 = jnp.float32, jnp.bfloat16
RIM = 512
NSUB = 4
TB = 256
WIN = TB + 2 * RIM
LANE = 128
NEVER = 64.0
FIELDS, LEVELS, COLS = 16, 8, 2048
REST = (LEVELS - 1) * FIELDS
WIDE = COLS - RIM
PICK_MIB = 63
EARLY = 4
PAY = 4 + 2 * WIDE // TB


def mix_kernel(
    state_hbm, rate_hbm, send_hbm, offs_hbm, coef_hbm, mask_hbm, couple_hbm, packed, mix0, mixr, tabs, gate,
    state, rate, send, offs, coef, mask, couple, sems,
):
    pairs = (
        (state_hbm.at[0, 0:2], state.at[0:2]),
        (rate_hbm, rate),
        (send_hbm, send),
        (offs_hbm, offs),
        (coef_hbm, coef),
        (mask_hbm, mask),
        (couple_hbm, couple),
        (state_hbm.at[0, 2:LEVELS], state.at[2:LEVELS]),
    )
    copies = [pltpu.make_async_copy(a, b, sems.at[i]) for i, (a, b) in enumerate(pairs)]
    for copy in copies:
        copy.start()
    for copy in copies[:3]:
        copy.wait()
    for c in range(0, COLS, TB):
        here = slice(c, c + TB)
        v0 = state[0, :, here]
        mix0[:, here] = v0 + rate[0, :, here] * (state[1, :, here] - v0)
    for k in range(5):
        for j in range(4):
            for h in range(2):
                index = send[k, j : j + 1, h * LANE : (h + 1) * LANE]
                low = jnp.broadcast_to(index & (LANE - 1), (FIELDS, LANE))
                high = jnp.broadcast_to(lax.shift_right_logical(index, 7), (FIELDS, LANE))
                total = jnp.zeros((FIELDS, LANE), F32)
                for p in range(COLS // LANE):
                    got = jnp.take_along_axis(
                        mix0[:, p * LANE : (p + 1) * LANE], low, axis=1, mode="promise_in_bounds"
                    )
                    total = jnp.where(high == p, got, total)
                packed[k, j, :, h * LANE : (h + 1) * LANE] = total.astype(BF16)
    for copy in copies[3:]:
        copy.wait()
    eye = lax.broadcasted_iota(jnp.int32, (FIELDS, FIELDS), 0) == lax.broadcasted_iota(
        jnp.int32, (FIELDS, FIELDS), 1
    )
    couple_column = jnp.sum(
        jnp.where(eye, jnp.broadcast_to(couple[...], (FIELDS, FIELDS)), 0.0), axis=1, keepdims=True
    )
    for n in range(COLS // TB):
        here = slice(n * TB, (n + 1) * TB)
        gate[:, here] = couple_column * mask[0:1, here].astype(F32)
        before = state[0, :, here]
        mid = state[1, :, here]
        flux = rate[0, :, here] * (mid - before)
        for l in range(1, LEVELS):
            if l < LEVELS - 1:
                after_mid = state[l + 1, :, here]
                below = rate[l, :, here] * (after_mid - mid)
                new = mid + below - flux
                flux, mid = below, after_mid
            else:
                new = mid - flux
            mixr[(l - 1) * FIELDS : l * FIELDS, here] = new
        lane = lax.broadcasted_iota(jnp.int32, (1, TB), 1) + RIM
        off = [offs[j, :, here] for j in range(6)]
        val = [coef[j, :, here] for j in range(6)]
        zero = jnp.zeros((1, TB), F32)
        rows_c, rows_h, rows_l = [], [], []
        for j in range(6):
            merged = val[j]
            repeated = zero
            for i in range(6):
                if i != j:
                    same = off[i] == off[j]
                    merged = merged + jnp.where(same, val[i], 0.0)
                    if i < j:
                        repeated = jnp.where(same, 1.0, repeated)
            place = off[j] + lane
            rows_c.append(jnp.where(repeated > 0.5, 0.0, merged))
            rows_h.append(jnp.where(repeated > 0.5, NEVER, lax.shift_right_logical(place, 7).astype(F32)))
            rows_l.append((place & (LANE - 1)).astype(F32))
        tabs[2 * n] = jnp.concatenate(rows_c + [zero] * 2 + rows_h + [zero] * 2, axis=0).astype(BF16)
        tabs[2 * n + 1] = jnp.concatenate(rows_l + [zero] * 10, axis=0).astype(BF16)


def parities():
    d = lax.axis_index("dom")
    return (d & 1) == 0, (d & 2) == 0


def hold_kernel(tabs, kept):
    kept[...] = tabs[...]


def stage_kernel(swapped, tabs, e1, o1, e2, o2):
    near, far = parities()
    e1[0:4] = swapped[jnp.where(near, 3, 1)]
    e1[4:PAY] = tabs[pl.ds(jnp.where(near, 2 * COLS // TB - (PAY - 4), 0), PAY - 4)]
    o1[0:4] = swapped[jnp.where(near, 1, 3)]
    o1[4:PAY] = tabs[pl.ds(jnp.where(near, 0, 2 * COLS // TB - (PAY - 4)), PAY - 4)]
    e2[...] = swapped[jnp.where(far, 4, 0)]
    o2[...] = swapped[jnp.where(far, 0, 4)]


def build_bands(tab, rel, band, into, count, tabs, start):
    rows = [
        (lax.broadcasted_iota(jnp.int32, (16, LANE), 0) + r).astype(F32).astype(BF16) for r in range(0, LANE, 16)
    ]

    @pl.loop(0, count)
    def _(b):
        first = tabs[start + 2 * b].astype(F32)
        second = tabs[start + 2 * b + 1].astype(F32)
        tab[0:8] = first[0:8]
        tab[8:16] = first[8:16] * float(LANE) + second[0:8]
        for half in range(TB // LANE):
            lanes = slice(half * LANE, (half + 1) * LANE)
            coefs = [jnp.broadcast_to(tab[j : j + 1, lanes], (16, LANE)).astype(BF16) for j in range(6)]
            first_row = half * LANE
            last_row = first_row + LANE + 2 * RIM
            if first_row:
                band[into + b, 0:first_row, lanes] = jnp.zeros((first_row, LANE), BF16)
            if last_row < WIN:
                band[into + b, last_row:WIN, lanes] = jnp.zeros((WIN - last_row, LANE), BF16)
            for base in range(first_row, last_row, LANE):
                slot = 8 * (half * (WIN // LANE) + base // LANE)
                rel[slot : slot + 8, :] = tab[8:16, lanes] - float(base)
                there = [
                    jnp.broadcast_to(rel[slot + j : slot + j + 1, :], (16, LANE)).astype(BF16) for j in range(6)
                ]
                for r in range(0, LANE, 16):
                    total = jnp.zeros((16, LANE), BF16)
                    for j in range(6):
                        total = jnp.where(there[j] == rows[r // 16], coefs[j], total)
                    band[into + b, base + r : base + r + 16, lanes] = total


def own_band_kernel(tabs, mixr, after, band, bulk, tab, rel):
    del after
    for c in range(0, COLS, TB):
        bulk[:, c : c + TB] = mixr[:, c : c + TB].astype(BF16)
    build_bands(tab, rel, band, 0, EARLY, tabs, 0)


def side_band_kernel(e1, tabs, o1, after, band, late, keep, tab, rel):
    del after
    near, _ = parities()
    side = WIDE // TB
    places = (
        (e1, 4, side, jnp.where(near, WIDE + COLS, 0)),
        (tabs, 0, COLS // TB, WIDE),
        (o1, 4, side, jnp.where(near, 0, WIDE + COLS)),
    )
    for ref, start, count, base in places:
        for b in range(count):
            coefs = ref[start + 2 * b].astype(F32)[0:8]
            at = base + b * TB
            at = at if isinstance(at, int) else pl.multiple_of(at, TB)
            keep[:, pl.ds(at, TB)] = 1.0 - jnp.sum(coefs, axis=0, keepdims=True)
    build_bands(tab, rel, band, 0, side, e1, 4)
    build_bands(tab, rel, band, side, side, o1, 4)
    build_bands(tab, rel, late, 0, COLS // TB - EARLY, tabs, 2 * EARLY)


def remap_kernel(live, source, e1, o1, e2, o2, swapped, weights, mix0, gate, after, forcing, top, top_half, got):
    del after
    near, far = parities()
    got[pl.ds(jnp.where(far, 0, 16), 4)] = e2[...]
    got[pl.ds(jnp.where(near, 4, 12), 4)] = e1[0:4]
    got[8:12] = swapped[2]
    got[pl.ds(jnp.where(near, 12, 4), 4)] = o1[0:4]
    got[pl.ds(jnp.where(far, 16, 0), 4)] = o2[...]
    ones = jnp.ones((16, TB), BF16)
    for n in range(COLS // TB):
        here = slice(n * TB, (n + 1) * TB)
        num = jnp.zeros((FIELDS, TB), F32)
        den = jnp.zeros((1, TB), F32)
        for m in range(2):
            q = source[m, n]
            valid = jnp.where((q & 3) < live[0, lax.shift_right_logical(q, 2)], 1.0, 0.0).astype(F32)
            rows = jnp.concatenate([got[q], ones], axis=0)
            both = lax.dot_general(
                rows, weights[n, m], (((1,), (1,)), ((), ())), preferred_element_type=F32
            )
            num = num + valid * both[0:FIELDS]
            den = den + valid * both[FIELDS : FIELDS + 1]
        value = num / jnp.maximum(den, 1.0)
        forcing[:, here] = value
        old = mix0[:, here]
        new = old + gate[:, here] * (value - old)
        top[:, here] = new
        top_half[:, here] = new.astype(BF16)


EDGE = WIDE // TB
OWN = COLS // TB


def part(blocks, source, bands, keep, old, new):
    for b, band in blocks:
        rows = source[:, b * TB : b * TB + WIN]
        at = slice(b * TB, (b + 1) * TB)
        new(b, old(b) * keep[:, at] + jnp.dot(rows, bands(band), preferred_element_type=F32))


def blocks_of(own, side, on_right):
    return [(EDGE + n, ("own", n)) for n in own] + [((EDGE + OWN if on_right else 0) + n, ("side", n)) for n in side]


def own_band(early, late, n):
    return early[n] if n < EARLY else late[n - EARLY]


def per_order(run):
    near, _ = parities()

    @pl.when(near)
    def _():
        run(True)

    @pl.when(jnp.logical_not(near))
    def _():
        run(False)


def begin_kernel(band_own, band_late, band_side, keep, mixr, bulk, bulk_e, top, top_half, top_e, st, xa, xb, x0):
    x0[0:FIELDS, COLS : 2 * COLS] = top_half[...]
    x0[FIELDS:, COLS : 2 * COLS] = bulk[...]

    def run(right):
        there = slice(2 * COLS, 3 * COLS) if right else slice(0, COLS)
        x0[0:FIELDS, there] = top_e[...]
        x0[FIELDS:, there] = bulk_e[...]

        def bands(band):
            return own_band(band_own, band_late, band[1]) if band[0] == "own" else band_side[band[1]]

        for step in range(1, NSUB):
            count = OWN - 2 * step
            own = range(2 * step, OWN) if right else range(0, count)
            side = range(0, count) if right else range(2 * step - 2, EDGE)
            dst = xa if step % 2 else xb

            def old(b):
                if step > 1:
                    return st[:, b * TB : (b + 1) * TB]
                if EDGE <= b < EDGE + OWN:
                    mine = slice((b - EDGE) * TB, (b - EDGE + 1) * TB)
                    return jnp.concatenate([top[:, mine], mixr[:, mine]], axis=0)
                return x0[:, RIM + b * TB : RIM + (b + 1) * TB].astype(F32)

            def new(b, value):
                st[:, b * TB : (b + 1) * TB] = value
                dst[:, RIM + b * TB : RIM + (b + 1) * TB] = value.astype(BF16)

            src = x0 if step == 1 else (xb if step % 2 else xa)
            part(blocks_of(own, side, right), src, bands, keep, old, new)

    per_order(run)


def finish_kernel(
    band_own, band_late, band_side, keep, mixr, bulk, bulk_o, top, top_half, top_o, st_in, xa_in, xb_in, out, st, xa, xb, x0, result,
    sems,
):
    x0[0:FIELDS, COLS : 2 * COLS] = top_half[...]
    x0[FIELDS:, COLS : 2 * COLS] = bulk[...]

    def run(right):
        there = slice(0, COLS) if right else slice(2 * COLS, 3 * COLS)
        x0[0:FIELDS, there] = top_o[...]
        x0[FIELDS:, there] = bulk_o[...]

        def bands(band):
            return own_band(band_own, band_late, band[1]) if band[0] == "own" else band_side[EDGE + band[1]]

        for step in range(1, NSUB):
            first = EDGE + (2 * step if right else OWN - 2 * step - 4)
            at = slice(RIM + first * TB, RIM + (first + 4) * TB)
            if step % 2:
                xa[:, at] = xa_in[:, at]
            else:
                xb[:, at] = xb_in[:, at]
        for step in range(1, NSUB + 1):
            own = range(0, 2 * step) if right else range(OWN - 2 * step, OWN)
            side = range(2 * step - 2, EDGE) if right else range(0, OWN - 2 * step)
            before = range(2 * step - 2, 2 * step) if right else range(OWN - 2 * step, OWN - 2 * step + 2)
            dst = xa if step % 2 else xb

            def old(b):
                n = b - EDGE
                if step > 1:
                    return (st_in if n in before else st)[:, b * TB : (b + 1) * TB]
                if 0 <= n < OWN:
                    mine = slice(n * TB, (n + 1) * TB)
                    return jnp.concatenate([top[:, mine], mixr[:, mine]], axis=0)
                return x0[:, RIM + b * TB : RIM + (b + 1) * TB].astype(F32)

            def new(b, value):
                if step == NSUB:
                    mine = slice((b - EDGE) * TB, (b - EDGE + 1) * TB)
                    result[:, mine] = value
                    pltpu.make_async_copy(result.at[:, mine], out.at[:, mine], sems.at[b - EDGE]).start()
                else:
                    st[:, b * TB : (b + 1) * TB] = value
                    dst[:, RIM + b * TB : RIM + (b + 1) * TB] = value.astype(BF16)

            src = x0 if step == 1 else (xb if step % 2 else xa)
            part(blocks_of(own, side, not right), src, bands, keep, old, new)

    per_order(run)
    for n in range(OWN):
        mine = slice(n * TB, (n + 1) * TB)
        pltpu.make_async_copy(result.at[:, mine], out.at[:, mine], sems.at[n]).wait()


def crossed(value):
    size = (lax.axis_size("comp"), lax.axis_size("dom"))
    pairs = [(s * size[1] + d, (1 - s) * size[1] + d) for s in range(size[0]) for d in range(size[1])]
    return lax.ppermute(value, ("comp", "dom"), pairs)


def paired(value, apart, odd):
    count = lax.axis_size("dom")
    pairs = [(d, (d + (apart if bool(d & apart) == odd else -apart)) % count) for d in range(count)]
    return lax.ppermute(value, "dom", pairs)


def spec(n):
    return [pl.BlockSpec(memory_space=pltpu.VMEM)] * n


ANYWHERE = pl.BlockSpec(memory_space=pl.ANY)
SCALARS = pl.BlockSpec(memory_space=pltpu.SMEM)


def params(mib):
    return pltpu.CompilerParams(vmem_limit_bytes=mib * 2**20)


def cost(us):
    return pl.CostEstimate(flops=us * 1_000_000_000, bytes_accessed=us * 3_000_000, transcendentals=0)


def shards(
    column_state, vert_rate, hor_offsets, hor_coef, open_mask, couple_rate, send_index, live_slots, block_source,
    remap_weight,
):
    shape = jax.ShapeDtypeStruct
    rate = vert_rate.transpose(1, 0, 2)
    packed, mix0, mixr, tabs, gate = pl.pallas_call(
        mix_kernel,
        out_shape=[
            shape((5, 4, FIELDS, TB), BF16),
            shape((FIELDS, COLS), F32),
            shape((REST, COLS), F32),
            shape((2 * COLS // TB, 16, TB), BF16),
            shape((FIELDS, COLS), F32),
        ],
        in_specs=[pl.BlockSpec(memory_space=pltpu.HBM)] * 7,
        out_specs=spec(5),
        scratch_shapes=[
            pltpu.VMEM((LEVELS, FIELDS, COLS), F32),
            pltpu.VMEM((LEVELS - 1, 1, COLS), F32),
            pltpu.VMEM((5, 4, TB), jnp.int32),
            pltpu.VMEM((6, 1, COLS), jnp.int32),
            pltpu.VMEM((6, 1, COLS), F32),
            pltpu.VMEM((1, COLS), jnp.int32),
            pltpu.VMEM((1, FIELDS), F32),
            pltpu.SemaphoreType.DMA((8,)),
        ],
        compiler_params=params(PICK_MIB),
        cost_estimate=cost(3),
        name="mix",
    )(
        column_state, rate, send_index[0, 0], hor_offsets.transpose(1, 0, 2), hor_coef.transpose(1, 0, 2), open_mask,
        couple_rate,
    )
    swapped = crossed(packed)

    tabs = pl.pallas_call(
        hold_kernel,
        out_shape=shape(tabs.shape, BF16),
        in_specs=spec(1),
        out_specs=spec(1)[0],
        compiler_params=params(4),
        cost_estimate=cost(1),
        name="hold",
    )(tabs)
    pair = shape((4, FIELDS, TB), BF16)
    payload = shape((PAY, 16, TB), BF16)
    e1, o1, e2, o2 = pl.pallas_call(
        stage_kernel,
        out_shape=[payload, payload, pair, pair],
        in_specs=spec(2),
        out_specs=spec(4),
        compiler_params=params(4),
        cost_estimate=cost(1),
        name="stage",
    )(swapped, tabs)
    staged = e1
    e1, e2, o1, o2 = paired(e1, 1, False), paired(e2, 2, False), paired(o1, 1, True), paired(o2, 2, True)

    tab = pltpu.VMEM((16, TB), F32)
    rel = pltpu.VMEM((16 * (WIN // LANE), LANE), F32)
    band_own, bulk = pl.pallas_call(
        own_band_kernel,
        out_shape=[shape((EARLY, WIN, TB), BF16), shape((REST, COLS), BF16)],
        in_specs=spec(2) + [ANYWHERE],
        out_specs=spec(2),
        scratch_shapes=[tab, rel],
        compiler_params=params(8),
        cost_estimate=cost(3),
        name="own_band",
    )(tabs, mixr, staged)
    bulk_first, e2 = lax.optimization_barrier((bulk, e2))
    bulk_o = paired(bulk_first, 1, True)
    bulk_then, e1 = lax.optimization_barrier((bulk, e1))
    bulk_e = paired(bulk_then, 1, False)

    forcing, top, top_half = pl.pallas_call(
        remap_kernel,
        out_shape=[shape((FIELDS, COLS), F32), shape((FIELDS, COLS), F32), shape((FIELDS, COLS), BF16)],
        in_specs=[SCALARS, SCALARS] + spec(8) + [ANYWHERE],
        out_specs=spec(3),
        scratch_shapes=[pltpu.VMEM((20, FIELDS, TB), BF16)],
        compiler_params=params(8),
        cost_estimate=cost(20),
        name="remap",
    )(
        live_slots[0], block_source[0, 0].T, e1, o1, e2, o2, swapped, remap_weight[0, 0], mix0, gate, band_own,
    )
    top_e, top_o = paired(top_half, 1, False), paired(top_half, 1, True)

    band_side, band_late, keep = pl.pallas_call(
        side_band_kernel,
        out_shape=[shape((2 * WIDE // TB, WIN, TB), BF16), shape((OWN - EARLY, WIN, TB), BF16), shape((1, COLS + 2 * WIDE), F32)],
        in_specs=spec(3) + [ANYWHERE],
        out_specs=spec(3),
        scratch_shapes=[tab, rel],
        compiler_params=params(8),
        cost_estimate=cost(1),
        name="side_band",
    )(e1, tabs, o1, top_half)

    wide = (LEVELS * FIELDS, 3 * COLS)
    narrow = (LEVELS * FIELDS, COLS + 2 * WIDE)
    st, xa, xb = pl.pallas_call(
        begin_kernel,
        out_shape=[shape(narrow, F32), shape(wide, BF16), shape(wide, BF16)],
        in_specs=spec(10),
        out_specs=spec(3),
        scratch_shapes=[pltpu.VMEM(wide, BF16)],
        compiler_params=params(8),
        cost_estimate=cost(1),
        name="begin",
    )(band_own, band_late, band_side, keep, mixr, bulk, bulk_e, top, top_half, top_e)
    state = pl.pallas_call(
        finish_kernel,
        out_shape=shape((LEVELS * FIELDS, COLS), F32),
        in_specs=spec(13),
        out_specs=ANYWHERE,
        scratch_shapes=[
            pltpu.VMEM(narrow, F32), pltpu.VMEM(wide, BF16), pltpu.VMEM(wide, BF16), pltpu.VMEM(wide, BF16),
            pltpu.VMEM((LEVELS * FIELDS, COLS), F32), pltpu.SemaphoreType.DMA((OWN,)),
        ],
        compiler_params=params(16),
        cost_estimate=cost(4),
        name="finish",
    )(band_own, band_late, band_side, keep, mixr, bulk, bulk_o, top, top_half, top_o, st, xa, xb)
    return state.reshape(1, LEVELS, FIELDS, COLS), forcing[None]


def solution(mesh):
    placed = (
        P("comp", None, None, "dom"),
        P("comp", None, "dom"),
        P("comp", None, "dom"),
        P("comp", None, "dom"),
        P("comp", "dom"),
        P("comp", None),
        P("comp", "dom", None, None, None),
        P("comp", "dom", None),
        P("comp", "dom", None, None),
        P("comp", "dom", None, None, None, None),
    )
    return jax.shard_map(
        shards,
        mesh=mesh,
        in_specs=placed,
        out_specs=(P("comp", None, None, "dom"), P("comp", None, "dom")),
        check_vma=False,
    )
```

```python
import jax
import jax.numpy as jnp
from jax import lax
from jax.experimental import pallas as pl
from jax.experimental.pallas import tpu as pltpu
from jax.sharding import PartitionSpec as P

F32, BF16 = jnp.float32, jnp.bfloat16
RIM = 512
NSUB = 4
TB = 256
WIN = TB + 2 * RIM
LANE = 128
NEVER = 64.0
FIELDS, LEVELS, COLS = 16, 8, 2048
REST = (LEVELS - 1) * FIELDS
WIDE = COLS - RIM
PICK_MIB = 63
EARLY = 6
PAY = 4 + 2 * WIDE // TB


def mix_kernel(
    state_hbm, rate_hbm, send_hbm, offs_hbm, coef_hbm, mask_hbm, couple_hbm, packed, mix0, mixr, tabs, gate,
    state, rate, send, offs, coef, mask, couple, sems,
):
    pairs = (
        (state_hbm.at[0, 0:2], state.at[0:2]),
        (rate_hbm, rate),
        (send_hbm, send),
        (offs_hbm, offs),
        (coef_hbm, coef),
        (mask_hbm, mask),
        (couple_hbm, couple),
        (state_hbm.at[0, 2:LEVELS], state.at[2:LEVELS]),
    )
    copies = [pltpu.make_async_copy(a, b, sems.at[i]) for i, (a, b) in enumerate(pairs)]
    for copy in copies:
        copy.start()
    for copy in copies[:3]:
        copy.wait()
    for c in range(0, COLS, TB):
        here = slice(c, c + TB)
        v0 = state[0, :, here]
        mix0[:, here] = v0 + rate[0, :, here] * (state[1, :, here] - v0)
    for k in range(5):
        for j in range(4):
            for h in range(2):
                index = send[k, j : j + 1, h * LANE : (h + 1) * LANE]
                low = jnp.broadcast_to(index & (LANE - 1), (FIELDS, LANE))
                high = jnp.broadcast_to(lax.shift_right_logical(index, 7), (FIELDS, LANE))
                total = jnp.zeros((FIELDS, LANE), F32)
                for p in range(COLS // LANE):
                    got = jnp.take_along_axis(
                        mix0[:, p * LANE : (p + 1) * LANE], low, axis=1, mode="promise_in_bounds"
                    )
                    total = jnp.where(high == p, got, total)
                packed[k, j, :, h * LANE : (h + 1) * LANE] = total.astype(BF16)
    for copy in copies[3:]:
        copy.wait()
    eye = lax.broadcasted_iota(jnp.int32, (FIELDS, FIELDS), 0) == lax.broadcasted_iota(
        jnp.int32, (FIELDS, FIELDS), 1
    )
    couple_column = jnp.sum(
        jnp.where(eye, jnp.broadcast_to(couple[...], (FIELDS, FIELDS)), 0.0), axis=1, keepdims=True
    )
    for n in range(COLS // TB):
        here = slice(n * TB, (n + 1) * TB)
        gate[:, here] = couple_column * mask[0:1, here].astype(F32)
        before = state[0, :, here]
        mid = state[1, :, here]
        flux = rate[0, :, here] * (mid - before)
        for l in range(1, LEVELS):
            if l < LEVELS - 1:
                after_mid = state[l + 1, :, here]
                below = rate[l, :, here] * (after_mid - mid)
                new = mid + below - flux
                flux, mid = below, after_mid
            else:
                new = mid - flux
            mixr[(l - 1) * FIELDS : l * FIELDS, here] = new
        lane = lax.broadcasted_iota(jnp.int32, (1, TB), 1) + RIM
        off = [offs[j, :, here] for j in range(6)]
        val = [coef[j, :, here] for j in range(6)]
        zero = jnp.zeros((1, TB), F32)
        rows_c, rows_h, rows_l = [], [], []
        for j in range(6):
            merged = val[j]
            repeated = zero
            for i in range(6):
                if i != j:
                    same = off[i] == off[j]
                    merged = merged + jnp.where(same, val[i], 0.0)
                    if i < j:
                        repeated = jnp.where(same, 1.0, repeated)
            place = off[j] + lane
            rows_c.append(jnp.where(repeated > 0.5, 0.0, merged))
            rows_h.append(jnp.where(repeated > 0.5, NEVER, lax.shift_right_logical(place, 7).astype(F32)))
            rows_l.append((place & (LANE - 1)).astype(F32))
        tabs[2 * n] = jnp.concatenate(rows_c + [zero] * 2 + rows_h + [zero] * 2, axis=0).astype(BF16)
        tabs[2 * n + 1] = jnp.concatenate(rows_l + [zero] * 10, axis=0).astype(BF16)


def parities():
    d = lax.axis_index("dom")
    return (d & 1) == 0, (d & 2) == 0


def hold_kernel(tabs, kept):
    kept[...] = tabs[...]


def stage_kernel(swapped, tabs, e1, o1, e2, o2):
    near, far = parities()
    e1[0:4] = swapped[jnp.where(near, 3, 1)]
    e1[4:PAY] = tabs[pl.ds(jnp.where(near, 2 * COLS // TB - (PAY - 4), 0), PAY - 4)]
    o1[0:4] = swapped[jnp.where(near, 1, 3)]
    o1[4:PAY] = tabs[pl.ds(jnp.where(near, 0, 2 * COLS // TB - (PAY - 4)), PAY - 4)]
    e2[...] = swapped[jnp.where(far, 4, 0)]
    o2[...] = swapped[jnp.where(far, 0, 4)]


def build_bands(tab, rel, band, into, count, tabs, start):
    rows = [
        (lax.broadcasted_iota(jnp.int32, (16, LANE), 0) + r).astype(F32).astype(BF16) for r in range(0, LANE, 16)
    ]

    @pl.loop(0, count)
    def _(b):
        first = tabs[start + 2 * b].astype(F32)
        second = tabs[start + 2 * b + 1].astype(F32)
        tab[0:8] = first[0:8]
        tab[8:16] = first[8:16] * float(LANE) + second[0:8]
        for half in range(TB // LANE):
            lanes = slice(half * LANE, (half + 1) * LANE)
            coefs = [jnp.broadcast_to(tab[j : j + 1, lanes], (16, LANE)).astype(BF16) for j in range(6)]
            first_row = half * LANE
            last_row = first_row + LANE + 2 * RIM
            if first_row:
                band[into + b, 0:first_row, lanes] = jnp.zeros((first_row, LANE), BF16)
            if last_row < WIN:
                band[into + b, last_row:WIN, lanes] = jnp.zeros((WIN - last_row, LANE), BF16)
            for base in range(first_row, last_row, LANE):
                slot = 8 * (half * (WIN // LANE) + base // LANE)
                rel[slot : slot + 8, :] = tab[8:16, lanes] - float(base)
                there = [
                    jnp.broadcast_to(rel[slot + j : slot + j + 1, :], (16, LANE)).astype(BF16) for j in range(6)
                ]
                for r in range(0, LANE, 16):
                    total = jnp.zeros((16, LANE), BF16)
                    for j in range(6):
                        total = jnp.where(there[j] == rows[r // 16], coefs[j], total)
                    band[into + b, base + r : base + r + 16, lanes] = total


def own_band_kernel(tabs, mixr, after, band, bulk, tab, rel):
    del after
    for c in range(0, COLS, TB):
        bulk[:, c : c + TB] = mixr[:, c : c + TB].astype(BF16)
    build_bands(tab, rel, band, 0, EARLY, tabs, 0)


def side_band_kernel(e1, tabs, o1, after, band, late, keep, tab, rel):
    del after
    near, _ = parities()
    side = WIDE // TB
    places = (
        (e1, 4, side, jnp.where(near, WIDE + COLS, 0)),
        (tabs, 0, COLS // TB, WIDE),
        (o1, 4, side, jnp.where(near, 0, WIDE + COLS)),
    )
    for ref, start, count, base in places:
        for b in range(count):
            coefs = ref[start + 2 * b].astype(F32)[0:8]
            at = base + b * TB
            at = at if isinstance(at, int) else pl.multiple_of(at, TB)
            keep[:, pl.ds(at, TB)] = 1.0 - jnp.sum(coefs, axis=0, keepdims=True)
    build_bands(tab, rel, band, 0, side, e1, 4)
    build_bands(tab, rel, band, side, side, o1, 4)
    build_bands(tab, rel, late, 0, COLS // TB - EARLY, tabs, 2 * EARLY)


def remap_kernel(live, source, e1, o1, e2, o2, swapped, weights, mix0, gate, after, forcing, top, top_half, got):
    del after
    near, far = parities()
    got[pl.ds(jnp.where(far, 0, 16), 4)] = e2[...]
    got[pl.ds(jnp.where(near, 4, 12), 4)] = e1[0:4]
    got[8:12] = swapped[2]
    got[pl.ds(jnp.where(near, 12, 4), 4)] = o1[0:4]
    got[pl.ds(jnp.where(far, 16, 0), 4)] = o2[...]
    ones = jnp.ones((16, TB), BF16)
    for n in range(COLS // TB):
        here = slice(n * TB, (n + 1) * TB)
        num = jnp.zeros((FIELDS, TB), F32)
        den = jnp.zeros((1, TB), F32)
        for m in range(2):
            q = source[m, n]
            valid = jnp.where((q & 3) < live[0, lax.shift_right_logical(q, 2)], 1.0, 0.0).astype(F32)
            rows = jnp.concatenate([got[q], ones], axis=0)
            both = lax.dot_general(
                rows, weights[n, m], (((1,), (1,)), ((), ())), preferred_element_type=F32
            )
            num = num + valid * both[0:FIELDS]
            den = den + valid * both[FIELDS : FIELDS + 1]
        value = num / jnp.maximum(den, 1.0)
        forcing[:, here] = value
        old = mix0[:, here]
        new = old + gate[:, here] * (value - old)
        top[:, here] = new
        top_half[:, here] = new.astype(BF16)


EDGE = WIDE // TB
OWN = COLS // TB


def part(blocks, source, bands, keep, old, new):
    for b, band in blocks:
        rows = source[:, b * TB : b * TB + WIN]
        at = slice(b * TB, (b + 1) * TB)
        new(b, old(b) * keep[:, at] + jnp.dot(rows, bands(band), preferred_element_type=F32))


def blocks_of(own, side, on_right):
    return [(EDGE + n, ("own", n)) for n in own] + [((EDGE + OWN if on_right else 0) + n, ("side", n)) for n in side]


def own_band(early, late, n):
    return early[n] if n < EARLY else late[n - EARLY]


def per_order(run):
    near, _ = parities()

    @pl.when(near)
    def _():
        run(True)

    @pl.when(jnp.logical_not(near))
    def _():
        run(False)


def begin_kernel(band_own, band_late, band_side, keep, mixr, bulk, bulk_e, top, top_half, top_e, st, xa, xb, x0):
    x0[0:FIELDS, COLS : 2 * COLS] = top_half[...]
    x0[FIELDS:, COLS : 2 * COLS] = bulk[...]

    def run(right):
        there = slice(2 * COLS, 3 * COLS) if right else slice(0, COLS)
        x0[0:FIELDS, there] = top_e[...]
        x0[FIELDS:, there] = bulk_e[...]

        def bands(band):
            return own_band(band_own, band_late, band[1]) if band[0] == "own" else band_side[band[1]]

        for step in range(1, NSUB):
            count = OWN - 2 * step
            own = range(2 * step, OWN) if right else range(0, count)
            side = range(0, count) if right else range(2 * step - 2, EDGE)
            dst = xa if step % 2 else xb

            def old(b):
                if step > 1:
                    return st[:, b * TB : (b + 1) * TB]
                if EDGE <= b < EDGE + OWN:
                    mine = slice((b - EDGE) * TB, (b - EDGE + 1) * TB)
                    return jnp.concatenate([top[:, mine], mixr[:, mine]], axis=0)
                return x0[:, RIM + b * TB : RIM + (b + 1) * TB].astype(F32)

            def new(b, value):
                st[:, b * TB : (b + 1) * TB] = value
                dst[:, RIM + b * TB : RIM + (b + 1) * TB] = value.astype(BF16)

            src = x0 if step == 1 else (xb if step % 2 else xa)
            part(blocks_of(own, side, right), src, bands, keep, old, new)

    per_order(run)


def finish_kernel(
    band_own, band_late, band_side, keep, mixr, bulk, bulk_o, top, top_half, top_o, st_in, xa_in, xb_in, out, st, xa, xb, x0, result,
    sems,
):
    x0[0:FIELDS, COLS : 2 * COLS] = top_half[...]
    x0[FIELDS:, COLS : 2 * COLS] = bulk[...]

    def run(right):
        there = slice(0, COLS) if right else slice(2 * COLS, 3 * COLS)
        x0[0:FIELDS, there] = top_o[...]
        x0[FIELDS:, there] = bulk_o[...]

        def bands(band):
            return own_band(band_own, band_late, band[1]) if band[0] == "own" else band_side[EDGE + band[1]]

        for step in range(1, NSUB):
            first = EDGE + (2 * step if right else OWN - 2 * step - 4)
            at = slice(RIM + first * TB, RIM + (first + 4) * TB)
            if step % 2:
                xa[:, at] = xa_in[:, at]
            else:
                xb[:, at] = xb_in[:, at]
        for step in range(1, NSUB + 1):
            own = range(0, 2 * step) if right else range(OWN - 2 * step, OWN)
            side = range(2 * step - 2, EDGE) if right else range(0, OWN - 2 * step)
            before = range(2 * step - 2, 2 * step) if right else range(OWN - 2 * step, OWN - 2 * step + 2)
            dst = xa if step % 2 else xb

            def old(b):
                n = b - EDGE
                if step > 1:
                    return (st_in if n in before else st)[:, b * TB : (b + 1) * TB]
                if 0 <= n < OWN:
                    mine = slice(n * TB, (n + 1) * TB)
                    return jnp.concatenate([top[:, mine], mixr[:, mine]], axis=0)
                return x0[:, RIM + b * TB : RIM + (b + 1) * TB].astype(F32)

            def new(b, value):
                if step == NSUB:
                    mine = slice((b - EDGE) * TB, (b - EDGE + 1) * TB)
                    result[:, mine] = value
                    pltpu.make_async_copy(result.at[:, mine], out.at[:, mine], sems.at[b - EDGE]).start()
                else:
                    st[:, b * TB : (b + 1) * TB] = value
                    dst[:, RIM + b * TB : RIM + (b + 1) * TB] = value.astype(BF16)

            src = x0 if step == 1 else (xb if step % 2 else xa)
            part(blocks_of(own, side, not right), src, bands, keep, old, new)

    per_order(run)
    for n in range(OWN):
        mine = slice(n * TB, (n + 1) * TB)
        pltpu.make_async_copy(result.at[:, mine], out.at[:, mine], sems.at[n]).wait()


def crossed(value):
    size = (lax.axis_size("comp"), lax.axis_size("dom"))
    pairs = [(s * size[1] + d, (1 - s) * size[1] + d) for s in range(size[0]) for d in range(size[1])]
    return lax.ppermute(value, ("comp", "dom"), pairs)


def paired(value, apart, odd):
    count = lax.axis_size("dom")
    pairs = [(d, (d + (apart if bool(d & apart) == odd else -apart)) % count) for d in range(count)]
    return lax.ppermute(value, "dom", pairs)


def spec(n):
    return [pl.BlockSpec(memory_space=pltpu.VMEM)] * n


ANYWHERE = pl.BlockSpec(memory_space=pl.ANY)
SCALARS = pl.BlockSpec(memory_space=pltpu.SMEM)


def params(mib):
    return pltpu.CompilerParams(vmem_limit_bytes=mib * 2**20)


def cost(us):
    return pl.CostEstimate(flops=us * 1_000_000_000, bytes_accessed=us * 3_000_000, transcendentals=0)


def shards(
    column_state, vert_rate, hor_offsets, hor_coef, open_mask, couple_rate, send_index, live_slots, block_source,
    remap_weight,
):
    shape = jax.ShapeDtypeStruct
    rate = vert_rate.transpose(1, 0, 2)
    packed, mix0, mixr, tabs, gate = pl.pallas_call(
        mix_kernel,
        out_shape=[
            shape((5, 4, FIELDS, TB), BF16),
            shape((FIELDS, COLS), F32),
            shape((REST, COLS), F32),
            shape((2 * COLS // TB, 16, TB), BF16),
            shape((FIELDS, COLS), F32),
        ],
        in_specs=[pl.BlockSpec(memory_space=pltpu.HBM)] * 7,
        out_specs=spec(5),
        scratch_shapes=[
            pltpu.VMEM((LEVELS, FIELDS, COLS), F32),
            pltpu.VMEM((LEVELS - 1, 1, COLS), F32),
            pltpu.VMEM((5, 4, TB), jnp.int32),
            pltpu.VMEM((6, 1, COLS), jnp.int32),
            pltpu.VMEM((6, 1, COLS), F32),
            pltpu.VMEM((1, COLS), jnp.int32),
            pltpu.VMEM((1, FIELDS), F32),
            pltpu.SemaphoreType.DMA((8,)),
        ],
        compiler_params=params(PICK_MIB),
        cost_estimate=cost(3),
        name="mix",
    )(
        column_state, rate, send_index[0, 0], hor_offsets.transpose(1, 0, 2), hor_coef.transpose(1, 0, 2), open_mask,
        couple_rate,
    )
    swapped = crossed(packed)

    tabs = pl.pallas_call(
        hold_kernel,
        out_shape=shape(tabs.shape, BF16),
        in_specs=spec(1),
        out_specs=spec(1)[0],
        compiler_params=params(4),
        cost_estimate=cost(1),
        name="hold",
    )(tabs)
    pair = shape((4, FIELDS, TB), BF16)
    payload = shape((PAY, 16, TB), BF16)
    e1, o1, e2, o2 = pl.pallas_call(
        stage_kernel,
        out_shape=[payload, payload, pair, pair],
        in_specs=spec(2),
        out_specs=spec(4),
        compiler_params=params(4),
        cost_estimate=cost(1),
        name="stage",
    )(swapped, tabs)
    staged = e1
    e1, e2, o1, o2 = paired(e1, 1, False), paired(e2, 2, False), paired(o1, 1, True), paired(o2, 2, True)

    tab = pltpu.VMEM((16, TB), F32)
    rel = pltpu.VMEM((16 * (WIN // LANE), LANE), F32)
    band_own, bulk = pl.pallas_call(
        own_band_kernel,
        out_shape=[shape((EARLY, WIN, TB), BF16), shape((REST, COLS), BF16)],
        in_specs=spec(2) + [ANYWHERE],
        out_specs=spec(2),
        scratch_shapes=[tab, rel],
        compiler_params=params(8),
        cost_estimate=cost(3),
        name="own_band",
    )(tabs, mixr, staged)
    bulk_later, e2 = lax.optimization_barrier((bulk, e2))
    bulk_e, bulk_o = paired(bulk_later, 1, False), paired(bulk_later, 1, True)

    forcing, top, top_half = pl.pallas_call(
        remap_kernel,
        out_shape=[shape((FIELDS, COLS), F32), shape((FIELDS, COLS), F32), shape((FIELDS, COLS), BF16)],
        in_specs=[SCALARS, SCALARS] + spec(8) + [ANYWHERE],
        out_specs=spec(3),
        scratch_shapes=[pltpu.VMEM((20, FIELDS, TB), BF16)],
        compiler_params=params(8),
        cost_estimate=cost(20),
        name="remap",
    )(
        live_slots[0], block_source[0, 0].T, e1, o1, e2, o2, swapped, remap_weight[0, 0], mix0, gate, band_own,
    )
    top_e, top_o = paired(top_half, 1, False), paired(top_half, 1, True)

    band_side, band_late, keep = pl.pallas_call(
        side_band_kernel,
        out_shape=[shape((2 * WIDE // TB, WIN, TB), BF16), shape((OWN - EARLY, WIN, TB), BF16), shape((1, COLS + 2 * WIDE), F32)],
        in_specs=spec(3) + [ANYWHERE],
        out_specs=spec(3),
        scratch_shapes=[tab, rel],
        compiler_params=params(8),
        cost_estimate=cost(1),
        name="side_band",
    )(e1, tabs, o1, top_half)

    wide = (LEVELS * FIELDS, 3 * COLS)
    narrow = (LEVELS * FIELDS, COLS + 2 * WIDE)
    st, xa, xb = pl.pallas_call(
        begin_kernel,
        out_shape=[shape(narrow, F32), shape(wide, BF16), shape(wide, BF16)],
        in_specs=spec(10),
        out_specs=spec(3),
        scratch_shapes=[pltpu.VMEM(wide, BF16)],
        compiler_params=params(8),
        cost_estimate=cost(1),
        name="begin",
    )(band_own, band_late, band_side, keep, mixr, bulk, bulk_e, top, top_half, top_e)
    state = pl.pallas_call(
        finish_kernel,
        out_shape=shape((LEVELS * FIELDS, COLS), F32),
        in_specs=spec(13),
        out_specs=ANYWHERE,
        scratch_shapes=[
            pltpu.VMEM(narrow, F32), pltpu.VMEM(wide, BF16), pltpu.VMEM(wide, BF16), pltpu.VMEM(wide, BF16),
            pltpu.VMEM((LEVELS * FIELDS, COLS), F32), pltpu.SemaphoreType.DMA((OWN,)),
        ],
        compiler_params=params(16),
        cost_estimate=cost(4),
        name="finish",
    )(band_own, band_late, band_side, keep, mixr, bulk, bulk_o, top, top_half, top_o, st, xa, xb)
    return state.reshape(1, LEVELS, FIELDS, COLS), forcing[None]


def solution(mesh):
    placed = (
        P("comp", None, None, "dom"),
        P("comp", None, "dom"),
        P("comp", None, "dom"),
        P("comp", None, "dom"),
        P("comp", "dom"),
        P("comp", None),
        P("comp", "dom", None, None, None),
        P("comp", "dom", None),
        P("comp", "dom", None, None),
        P("comp", "dom", None, None, None, None),
    )
    return jax.shard_map(
        shards,
        mesh=mesh,
        in_specs=placed,
        out_specs=(P("comp", None, None, "dom"), P("comp", None, "dom")),
        check_vma=False,
    )
```
